768 devices in a mesh: gx: 96 (over z, x, core), gy: 8 (over y).
Axes of the slice: x: 4, y: 8, z: 12, core: 2. Of those that a mesh axis runs over, the one named last changes fastest.
Arguments:
- recharge: float32 [48, 768, 1024], P(None, 'gx', 'gy'), as said below
- conduct: float32 [48, 768, 1024], P(None, 'gx', 'gy'), may hold values from 0.1 to 10
- top_layer: int32 [768, 1024], P('gx', 'gy'), may hold values from 0 to 24
- fixed_head: int32 [768, 1024], P('gx', 'gy'), may hold values 0 or 1
Outputs:
- head_field: float32 [48, 768, 1024], P(None, 'gx', 'gy')
- residual: float32 [48, 768, 1024], P(None, 'gx', 'gy')
- applied: float32 [48, 768, 1024], P(None, 'gx', 'gy')
The draws below stay inside these ranges and needn't reach their ends.
Inputs may be any that keep to these rules, and one draw needn't show every extreme that they name: `recharge`: recharge is of order one and its magnitude varies from column to column.
All inputs are finite; a program needn't handle non-finite values. No bound on the sum of `fixed_head` on one device may be relied on, other than what follows from the above.
Results may differ from the reference program's by a relative error of at most 0.0038.
Values sent between devices are 32-bit elements; how exact they have to be, the bound alone decides.
No kernel may reach another device: no remote copies, remote signals or barrier semaphores. Data moves between devices by JAX's collectives and lax.ppermute only.
A program may use at most 64 MiB of HBM per device.

```python
import math
import jax
import jax.numpy as jnp
from jax import lax

LAYERS = 48
ITERS = 4
NX = 768
NY = 1024


def draw_recharge(key, part):
    key = jax.random.fold_in(key, 11)
    first_key = jax.random.fold_in(key, 0)
    column = jnp.arange(NX, dtype=jnp.float32)
    rising = jnp.sqrt(1.0 + 2.0 * column / max(NX - 1, 1))[None, :, None]
    rough = jax.random.normal(first_key, (LAYERS, NX, NY), jnp.float32)
    return (rough * rising).astype(jnp.float32)


def with_ends(drawn, own_key, low, largest):
    longest = drawn.shape.index(max(drawn.shape))
    spots = []
    for shift in (0, 1):
        where = [jax.random.randint(jax.random.fold_in(own_key, axis), (), 0, length) for axis, length in enumerate(drawn.shape)]
        where[longest] = (where[longest] + shift) % drawn.shape[longest]
        spots.append(tuple(where))
    return drawn.at[spots[0]].set(low).at[spots[1]].set(largest)


def block_levels(stream_key, extent, cuts, low, high):
    loudness, own = 1.0, jax.random.fold_in(stream_key, 6)
    for position, parts in cuts:
        draws = jnp.exp(jax.random.uniform(jax.random.fold_in(own, position), (parts,), jnp.float32, low / len(cuts), high / len(cuts)))
        loudness = loudness * jnp.repeat(draws, extent[position] // parts).reshape([-1 if axis == position else 1 for axis in range(len(extent))])
    return loudness


def setup_inputs(seed: int = 0) -> dict:
    key_list = jax.random.split(jax.random.key(seed), 5)
    recharge = draw_recharge(jax.random.fold_in(key_list[4], 71), 0)
    conduct = jnp.clip(jnp.exp(math.log(10.0) - 4.6051702 * jax.random.uniform(key_list[1], (LAYERS, NX, NY), jnp.float32) ** block_levels(key_list[1], (LAYERS, NX, NY), ((1, 96), (2, 8)), -0.2, 0.2)), 0.1, 10.0)
    top_layer = with_ends(jax.random.randint(key_list[2], (NX, NY), 0, LAYERS // 2 + 1), jax.random.fold_in(key_list[2], 1), 0, (LAYERS // 2 + 1) - 1).astype(jnp.int32)
    fixed_head = with_ends((jax.random.randint(key_list[3], (NX, NY), 0, 4) < 1).astype(jnp.int32), jax.random.fold_in(key_list[3], 1), 0, 1)
    return {"recharge": recharge, "conduct": conduct, "top_layer": top_layer, "fixed_head": fixed_head}


store_term = 0.1
boundary_term = 4.0
vertical_ratio = 0.3

def face_coefficients(cond_pad):
    center = cond_pad[1:-1, 1:-1, 1:-1]
    east_c = jnp.sqrt(center * cond_pad[1:-1, 2:, 1:-1])
    west_c = jnp.sqrt(center * cond_pad[1:-1, :-2, 1:-1])
    north_c = jnp.sqrt(center * cond_pad[1:-1, 1:-1, 2:])
    south_c = jnp.sqrt(center * cond_pad[1:-1, 1:-1, :-2])
    upper_c = vertical_ratio * jnp.sqrt(center * cond_pad[2:, 1:-1, 1:-1])
    lower_c = vertical_ratio * jnp.sqrt(center * cond_pad[:-2, 1:-1, 1:-1])
    return (east_c, west_c, north_c, south_c, upper_c, lower_c)

def operate(padded, coeffs, diagonal):
    east_c, west_c, north_c, south_c, upper_c, lower_c = coeffs
    beside = east_c * padded[1:-1, 2:, 1:-1] + west_c * padded[1:-1, :-2, 1:-1]
    beside = beside + north_c * padded[1:-1, 1:-1, 2:] + south_c * padded[1:-1, 1:-1, :-2]
    beside = beside + upper_c * padded[2:, 1:-1, 1:-1] + lower_c * padded[:-2, 1:-1, 1:-1]
    return diagonal * padded[1:-1, 1:-1, 1:-1] - beside

def reference(recharge, conduct, top_layer, fixed_head):
    level = lax.broadcasted_iota(jnp.int32, recharge.shape, 0)
    active = (level >= top_layer[None]).astype(jnp.float32)
    head_cell = ((level == top_layer[None]) & (fixed_head[None] == 1)).astype(jnp.float32)
    active_cond = conduct * active
    coeffs = face_coefficients(jnp.pad(active_cond, 1))
    total = coeffs[0] + coeffs[1] + coeffs[2] + coeffs[3] + coeffs[4] + coeffs[5]
    diagonal = active * (total + store_term + boundary_term * head_cell) + (1.0 - active)
    inverse = 1.0 / diagonal

    def apply_op(field):
        return operate(jnp.pad(field, 1), coeffs, diagonal)
    head_field = jnp.zeros_like(recharge)
    residual = recharge * active
    precond = inverse * residual
    applied = apply_op(precond)
    dir_image = jnp.zeros_like(recharge)
    dir_scaled = jnp.zeros_like(recharge)
    dir_applied = jnp.zeros_like(recharge)
    direction = jnp.zeros_like(recharge)
    gamma_old = jnp.float32(1.0)
    alpha_old = jnp.float32(1.0)
    for step in range(ITERS):
        gamma_now = jnp.sum(residual * precond)
        delta_now = jnp.sum(applied * precond)
        scaled = inverse * applied
        image = apply_op(scaled)
        if step == 0:
            beta_now = jnp.float32(0.0)
            alpha_now = gamma_now / delta_now
        else:
            beta_now = gamma_now / gamma_old
            alpha_now = gamma_now / (delta_now - beta_now * gamma_now / alpha_old)
        dir_image = image + beta_now * dir_image
        dir_scaled = scaled + beta_now * dir_scaled
        dir_applied = applied + beta_now * dir_applied
        direction = precond + beta_now * direction
        head_field = head_field + alpha_now * direction
        residual = residual - alpha_now * dir_applied
        precond = precond - alpha_now * dir_scaled
        applied = applied - alpha_now * dir_image
        gamma_old = gamma_now
        alpha_old = alpha_now
    return (head_field, residual, applied)
```

```python
import jax
import jax.numpy as jnp
from jax import lax
from jax.experimental import pallas as pl
from jax.experimental.pallas import tpu as pltpu
from jax.sharding import Mesh, PartitionSpec as P

ITERS = 4
LAYERS = 48
ROWS = 8
LANES = 128
SLOTS = 16
PACKED = 7
PLANES = 2 * LAYERS + 1
TALL = 3 * ROWS
MID = 2 * ROWS
BASIS = ITERS + 2

store_term = 0.1
boundary_term = 4.0
vertical_ratio = 0.3

GX = ("z", "x", "c")


def lane_index(rows):
    return lax.broadcasted_iota(jnp.int32, (rows, LANES), 1)


def pack_kernel(recharge, conduct, top_layer, fixed_head, fields, low_edge, high_edge):
    slot = lane_index(ROWS) // 8
    top = top_layer[...]

    def edges(tile, planes):
        low = jnp.zeros((ROWS, LANES), jnp.float32)
        high = jnp.zeros((ROWS, LANES), jnp.float32)
        for m, plane in enumerate(planes):
            turned = plane if m == 0 else pltpu.roll(plane, 8 * m, 1)
            low = jnp.where(slot == m, turned, low)
            high = jnp.where(slot == (m - 1) % SLOTS, turned, high)
        low_edge[tile] = low
        high_edge[tile] = high

    def group(k, _):
        roots, sources = [], []
        for m in range(SLOTS):
            level = k * SLOTS + m
            root = jnp.where(level >= top, jnp.sqrt(conduct[level]), 0.0)
            source = root * recharge[level]
            fields[level] = root
            fields[LAYERS + level] = source
            roots.append(root)
            sources.append(source)
        edges(k, roots)
        edges(LAYERS // SLOTS + k, sources)
        return 0

    lax.fori_loop(0, LAYERS // SLOTS, group, 0)
    fixed = fixed_head[...].astype(jnp.float32)
    fields[2 * LAYERS] = fixed
    edges(PACKED - 1, [fixed])


def beside(center, halo):
    lane = lane_index(center.shape[0])
    c_up, h_up = pltpu.roll(center, LANES - 1, 1), pltpu.roll(halo, LANES - 1, 1)
    c_down, h_down = pltpu.roll(center, 1, 1), pltpu.roll(halo, 1, 1)
    last, first = lane == LANES - 1, lane == 0
    c_sum = jnp.where(last, h_up, c_up) + jnp.where(first, h_down, c_down)
    h_sum = jnp.where(last, c_up, h_up) + jnp.where(first, c_down, h_down)
    return c_sum, h_sum


def around(c_ref, h_ref, base, height, rows):
    c_sum, h_sum = beside(c_ref[pl.ds(base, rows)], h_ref[pl.ds(base, rows)])

    def rest(ref):
        across = ref[pl.ds(base - 1, rows)] + ref[pl.ds(base + 1, rows)]
        vertical = ref[pl.ds(base - height, rows)] + ref[pl.ds(base + height, rows)]
        return across + vertical_ratio * vertical

    return c_sum + rest(c_ref), h_sum + rest(h_ref)


def basis_kernel(own, low, high, basis, inv_root, scale, moments,
                 s_c, s_h, q_c, q_h, f_c, f_h, g_c, g_h, diag, t0_c, t0_h, t_c, t_h):
    lane = lane_index(ROWS)
    rim = (lane < 8) | (lane >= LANES - 8)

    for ref, height in ((s_c, TALL), (s_h, TALL), (t0_c, TALL), (t0_h, TALL)):
        ref[pl.ds(0, height)] = jnp.zeros((height, LANES), jnp.float32)
        ref[pl.ds((LAYERS + 1) * height, height)] = jnp.zeros((height, LANES), jnp.float32)
    for j in range(ITERS):
        for ref in (t_c, t_h):
            ref[j, pl.ds(0, MID)] = jnp.zeros((MID, LANES), jnp.float32)
            ref[j, pl.ds((LAYERS + 1) * MID, MID)] = jnp.zeros((MID, LANES), jnp.float32)

    def halo_lanes(source, tile, m):
        both = jnp.where(lane // 8 == m, source[PLANES + tile], source[PLANES + PACKED + tile])
        turned = both if m == 0 else pltpu.roll(both, LANES - 8 * m, 1)
        return jnp.where(rim, turned, 0.0)

    for part, source in enumerate((low, own, high)):
        def assemble(k, _, source=source, part=part):
            for m in range(SLOTS):
                level = k * SLOTS + m
                row = pl.multiple_of(level * TALL, 8) + part * ROWS
                s_c[pl.ds(row + TALL, ROWS)] = source[level]
                q_c[pl.ds(row, ROWS)] = source[LAYERS + level]
                s_h[pl.ds(row + TALL, ROWS)] = halo_lanes(source, k, m)
                q_h[pl.ds(row, ROWS)] = halo_lanes(source, LAYERS // SLOTS + k, m)
            return 0

        lax.fori_loop(0, LAYERS // SLOTS, assemble, 0)
        f_c[pl.ds(part * ROWS, ROWS)] = boundary_term * source[2 * LAYERS]
        f_h[pl.ds(part * ROWS, ROWS)] = boundary_term * halo_lanes(source, PACKED - 1, 0)

    def first(level, _):
        here = pl.multiple_of(level * TALL, 8)
        base = here + TALL
        sums = around(s_c, s_h, base, TALL, TALL)
        outs = ((s_c, q_c, f_c, g_c, t0_c), (s_h, q_h, f_h, g_h, t0_h))
        for n, (s, q, f, g, t) in enumerate(outs):
            root = s[pl.ds(base, TALL)]
            above = s[pl.ds(base - TALL, TALL)]
            active = root > 0.0
            fixed = jnp.where(above > 0.0, 0.0, f[...])
            d = jnp.where(active, root * sums[n] + (store_term + fixed), 1.0)
            inverse = 1.0 / d
            g[pl.ds(here, TALL)] = root * root * inverse
            t[pl.ds(base, TALL)] = q[pl.ds(here, TALL)] * inverse
            if n == 0:
                diag[level] = d[ROWS:MID]
        return 0

    lax.fori_loop(0, LAYERS, first, 0)

    lead = ROWS // 2

    def second(level, _):
        base = pl.multiple_of((level + 1) * TALL, 8) + lead
        sums = around(t0_c, t0_h, base, TALL, MID)
        to = pl.multiple_of((level + 1) * MID, 8)
        t_c[0, pl.ds(to, MID)] = g_c[pl.ds(base - TALL, MID)] * sums[0]
        t_h[0, pl.ds(to, MID)] = g_h[pl.ds(base - TALL, MID)] * sums[1]
        return 0

    lax.fori_loop(0, LAYERS, second, 0)

    for j in range(1, ITERS):
        def later(level, _, j=j):
            base = pl.multiple_of((level + 1) * MID, 8)
            from_g = pl.multiple_of(level * TALL, 8) + lead
            sums = around(t_c.at[j - 1], t_h.at[j - 1], base, MID, MID)
            if j == 1:
                start = pl.multiple_of((level + 1) * TALL, 8) + lead
                before = t0_c[pl.ds(start, MID)], t0_h[pl.ds(start, MID)]
            else:
                before = t_c[j - 2, pl.ds(base, MID)], t_h[j - 2, pl.ds(base, MID)]
            t_c[j, pl.ds(base, MID)] = 2.0 * g_c[pl.ds(from_g, MID)] * sums[0] - before[0]
            t_h[j, pl.ds(base, MID)] = 2.0 * g_h[pl.ds(from_g, MID)] * sums[1] - before[1]
            return 0

        lax.fori_loop(0, LAYERS, later, 0)

    def last(level, totals):
        base = pl.multiple_of((level + 1) * MID, 8) + lead
        tall = pl.multiple_of(level * TALL, 8) + ROWS
        sums = around(t_c.at[ITERS - 1], t_h.at[ITERS - 1], base, MID, ROWS)
        t = [t0_c[pl.ds(tall + TALL, ROWS)]] + [t_c[j, pl.ds(base, ROWS)] for j in range(ITERS)]
        t.append(2.0 * g_c[pl.ds(tall, ROWS)] * sums[0] - t[ITERS - 1])
        for j in range(BASIS):
            basis[j, level] = t[j]
        root = s_c[pl.ds(tall + TALL, ROWS)]
        inv = jnp.where(root > 0.0, 1.0 / root, 0.0)
        ratio = diag[level] * inv
        inv_root[level] = inv
        scale[level] = ratio
        weight = ratio * inv
        out = []
        for j in range(ITERS):
            weighted = weight * t[j]
            out += [totals[2 * j] + weighted * t[j], totals[2 * j + 1] + weighted * t[j + 1]]
        return tuple(out)

    zero = jnp.zeros((ROWS, LANES), jnp.float32)
    totals = lax.fori_loop(0, LAYERS, last, (zero,) * (2 * ITERS))
    column = lane_index(1)
    row = jnp.zeros((1, LANES), jnp.float32)
    for n, total in enumerate(totals):
        row = jnp.where(column == n, jnp.sum(jnp.sum(total, axis=0, keepdims=True), axis=1, keepdims=True), row)
    moments[...] = row


def added(a, b, factor):
    out = []
    for i in range(max(len(a), len(b))):
        left = a[i] if i < len(a) else None
        right = b[i] if i < len(b) else None
        if right is not None:
            right = factor * right
        out.append(right if left is None else left if right is None else left + right)
    return out


def shifted(a):
    out = [None] * (len(a) + 1)

    def put(i, value):
        out[i] = value if out[i] is None else out[i] + value

    for i, value in enumerate(a):
        if i == 0:
            put(1, value)
        else:
            put(i + 1, 0.5 * value)
            put(i - 1, 0.5 * value)
    return out


def form(a, b, gram):
    total = None
    for i, left in enumerate(a):
        inner = None
        for j, right in enumerate(b):
            if right is None:
                continue
            term = right * gram(i, j)
            inner = term if inner is None else inner + term
        inner = left * inner
        total = inner if total is None else total + inner
    return total


def recursion(moments):
    half = [0.5 * m for m in moments]

    def gram(i, j):
        return moments[i] if j == 0 else moments[j] if i == 0 else half[i + j] + half[abs(i - j)]

    one = jnp.ones_like(moments[0])
    precond, direction, head = [one], [], []
    gamma_old = alpha_old = None
    for step in range(ITERS):
        gamma = form(precond, precond, gram)
        delta = gamma - form(precond, shifted(precond), gram)
        if step == 0:
            direction = precond
            alpha = gamma / delta
        else:
            beta = gamma / gamma_old
            alpha = gamma / (delta - beta * gamma / alpha_old)
            direction = added(precond, direction, beta)
        head = added(head, direction, alpha)
        moved = added(direction, shifted(direction), -1.0)
        precond = added(precond, moved, -alpha)
        gamma_old, alpha_old = gamma, alpha
    return head, precond, added(precond, shifted(precond), -1.0)


def combine_kernel(moments, basis, inv_root, scale, head_field, residual, applied):
    row = jnp.sum(moments[...], axis=0)
    column = lane_index(1)
    raw = []
    for n in range(2 * ITERS):
        value = jnp.sum(jnp.where(column == n, row, 0.0), axis=1, keepdims=True)
        raw.append(jnp.broadcast_to(value, (ROWS, LANES)))
    full = raw[:2]
    for n in range(2, 2 * ITERS):
        full.append(2.0 * raw[n] - raw[n % 2])
    coefficients = recursion(full)

    def write(level, _):
        t = [basis[j, level] for j in range(BASIS)]
        outs = []
        for weights in coefficients:
            total = weights[0] * t[0]
            for j in range(1, len(weights)):
                total = total + weights[j] * t[j]
            outs.append(total)
        factor = scale[level]
        head_field[level] = inv_root[level] * outs[0]
        residual[level] = factor * outs[1]
        applied[level] = factor * outs[2]
        return 0

    lax.fori_loop(0, LAYERS, write, 0)


def f32(*shape):
    return jax.ShapeDtypeStruct(shape, jnp.float32)


def scratch(*shape):
    return pltpu.VMEM(shape, jnp.float32)


def call(kernel, outs, scratches=()):
    whole = pl.BlockSpec(memory_space=pltpu.VMEM)
    return pl.pallas_call(
        kernel,
        out_shape=outs,
        out_specs=[whole] * len(outs),
        scratch_shapes=list(scratches),
        compiler_params=pltpu.CompilerParams(vmem_limit_bytes=32 * 1024 * 1024),
    )


def shift_both(low_going, high_going, axis):
    count = lax.axis_size(axis)
    up = [(i, i + 1) for i in range(count - 1)]
    down = [(target, source) for source, target in up]
    return lax.ppermute(high_going, axis, up), lax.ppermute(low_going, axis, down)


def spread_sum(row, axes):
    count = lax.axis_size(axes)
    got = lax.all_to_all(jnp.broadcast_to(row[None], (count,) + row.shape), axes, 0, 0, tiled=True)
    return got


def local(recharge, conduct, top_layer, fixed_head):
    tile = (ROWS, LANES)
    fields, low_edge, high_edge = call(
        pack_kernel,
        (f32(PLANES + 2 * PACKED, *tile), f32(PACKED, *tile), f32(PACKED, *tile)),
    )(recharge, conduct, top_layer, fixed_head)
    from_low, from_high = shift_both(low_edge, high_edge, "y")
    fields = lax.dynamic_update_slice(fields, jnp.concatenate([from_high, from_low], axis=0), (PLANES, 0, 0))
    low, high = shift_both(fields, fields, GX)

    tall, mid = (LAYERS + 2) * TALL, (LAYERS + 2) * MID
    basis, inv_root, scale, moments = call(
        basis_kernel,
        (f32(BASIS, LAYERS, *tile), f32(LAYERS, *tile), f32(LAYERS, *tile), f32(1, LANES)),
        [scratch(tall, LANES)] * 2 + [scratch(LAYERS * TALL, LANES)] * 2 + [scratch(TALL, LANES)] * 2
        + [scratch(LAYERS * TALL, LANES)] * 2 + [scratch(LAYERS, *tile)] + [scratch(tall, LANES)] * 2
        + [scratch(ITERS, mid, LANES)] * 2,
    )(fields, low, high)

    moments = jnp.sum(spread_sum(moments, ("z", "c")), axis=0)
    moments = spread_sum(moments, ("x", "y"))
    out = f32(LAYERS, *tile)
    return call(combine_kernel, (out, out, out))(moments, basis, inv_root, scale)


def solution(mesh):
    grid = Mesh(mesh.devices.reshape(12, 4, 2, 8), ("z", "x", "c", "y"))
    field, plane = P(None, GX, "y"), P(GX, "y")
    return jax.shard_map(
        local, mesh=grid, in_specs=(field, field, plane, plane), out_specs=(field, field, field), check_vma=False
    )
```

```python
import jax
import jax.numpy as jnp
from jax import lax
from jax.experimental import pallas as pl
from jax.experimental.pallas import tpu as pltpu
from jax.sharding import Mesh, PartitionSpec as P

ITERS = 4
LAYERS = 48
ROWS = 8
LANES = 128
SLOTS = 16
PACKED = 7
PLANES = 2 * LAYERS + 1
TALL = 3 * ROWS
MID = 2 * ROWS
BASIS = ITERS + 2

store_term = 0.1
boundary_term = 4.0
vertical_ratio = 0.3

GX = ("z", "x", "c")


def lane_index(rows):
    return lax.broadcasted_iota(jnp.int32, (rows, LANES), 1)


def pack_kernel(recharge, conduct, top_layer, fixed_head, fields, low_edge, high_edge):
    slot = lane_index(ROWS) // 8
    top = top_layer[...]

    def edges(tile, planes):
        low = jnp.zeros((ROWS, LANES), jnp.float32)
        high = jnp.zeros((ROWS, LANES), jnp.float32)
        for m, plane in enumerate(planes):
            turned = plane if m == 0 else pltpu.roll(plane, 8 * m, 1)
            low = jnp.where(slot == m, turned, low)
            high = jnp.where(slot == (m - 1) % SLOTS, turned, high)
        low_edge[tile] = low
        high_edge[tile] = high

    def group(k, _):
        roots, sources = [], []
        for m in range(SLOTS):
            level = k * SLOTS + m
            root = jnp.where(level >= top, jnp.sqrt(conduct[level]), 0.0)
            source = root * recharge[level]
            fields[level] = root
            fields[LAYERS + level] = source
            roots.append(root)
            sources.append(source)
        edges(k, roots)
        edges(LAYERS // SLOTS + k, sources)
        return 0

    lax.fori_loop(0, LAYERS // SLOTS, group, 0)
    fixed = fixed_head[...].astype(jnp.float32)
    fields[2 * LAYERS] = fixed
    edges(PACKED - 1, [fixed])


def beside(center, halo):
    lane = lane_index(center.shape[0])
    c_up, h_up = pltpu.roll(center, LANES - 1, 1), pltpu.roll(halo, LANES - 1, 1)
    c_down, h_down = pltpu.roll(center, 1, 1), pltpu.roll(halo, 1, 1)
    last, first = lane == LANES - 1, lane == 0
    c_sum = jnp.where(last, h_up, c_up) + jnp.where(first, h_down, c_down)
    h_sum = jnp.where(last, c_up, h_up) + jnp.where(first, c_down, h_down)
    return c_sum, h_sum


def around(c_ref, h_ref, base, height, rows):
    c_sum, h_sum = beside(c_ref[pl.ds(base, rows)], h_ref[pl.ds(base, rows)])

    def rest(ref):
        across = ref[pl.ds(base - 1, rows)] + ref[pl.ds(base + 1, rows)]
        vertical = ref[pl.ds(base - height, rows)] + ref[pl.ds(base + height, rows)]
        return across + vertical_ratio * vertical

    return c_sum + rest(c_ref), h_sum + rest(h_ref)


def put(stores):
    for ref, where, value in stores:
        ref[where] = value


def over_layers(step, unroll):
    def block(k, _):
        stores = []
        for m in range(unroll):
            stores += step(k * unroll + m)
        put(stores)
        return 0

    lax.fori_loop(0, LAYERS // unroll, block, 0)


def basis_kernel(own, low, high, basis, inv_root, scale, moments,
                 s_c, s_h, q_c, q_h, f_c, f_h, g_c, g_h, diag, t0_c, t0_h, *t_refs):
    t_c, t_h = t_refs[:ITERS], t_refs[ITERS:]
    lane = lane_index(ROWS)
    rim = (lane < 8) | (lane >= LANES - 8)

    for ref, height in ((s_c, TALL), (s_h, TALL), (t0_c, TALL), (t0_h, TALL)):
        ref[pl.ds(0, height)] = jnp.zeros((height, LANES), jnp.float32)
        ref[pl.ds((LAYERS + 1) * height, height)] = jnp.zeros((height, LANES), jnp.float32)
    for j in range(ITERS):
        for ref in (t_c[j], t_h[j]):
            ref[pl.ds(0, MID)] = jnp.zeros((MID, LANES), jnp.float32)
            ref[pl.ds((LAYERS + 1) * MID, MID)] = jnp.zeros((MID, LANES), jnp.float32)

    def halo_lanes(source, tile, m):
        both = jnp.where(lane // 8 == m, source[PLANES + tile], source[PLANES + PACKED + tile])
        turned = both if m == 0 else pltpu.roll(both, LANES - 8 * m, 1)
        return jnp.where(rim, turned, 0.0)

    for part, source in enumerate((low, own, high)):
        def assemble(k, _, source=source, part=part):
            for m in range(SLOTS):
                level = k * SLOTS + m
                row = pl.multiple_of(level * TALL, 8) + part * ROWS
                s_c[pl.ds(row + TALL, ROWS)] = source[level]
                q_c[pl.ds(row, ROWS)] = source[LAYERS + level]
                s_h[pl.ds(row + TALL, ROWS)] = halo_lanes(source, k, m)
                q_h[pl.ds(row, ROWS)] = halo_lanes(source, LAYERS // SLOTS + k, m)
            return 0

        lax.fori_loop(0, LAYERS // SLOTS, assemble, 0)
        f_c[pl.ds(part * ROWS, ROWS)] = boundary_term * source[2 * LAYERS]
        f_h[pl.ds(part * ROWS, ROWS)] = boundary_term * halo_lanes(source, PACKED - 1, 0)

    def first(level):
        here = pl.multiple_of(level * TALL, 8)
        base = here + TALL
        sums = around(s_c, s_h, base, TALL, TALL)
        stores = []
        outs = ((s_c, q_c, f_c, g_c, t0_c), (s_h, q_h, f_h, g_h, t0_h))
        for n, (s, q, f, g, t) in enumerate(outs):
            root = s[pl.ds(base, TALL)]
            above = s[pl.ds(base - TALL, TALL)]
            active = root > 0.0
            fixed = jnp.where(above > 0.0, 0.0, f[...])
            d = jnp.where(active, root * sums[n] + (store_term + fixed), 1.0)
            inverse = 1.0 / d
            stores.append((g, (pl.ds(here, TALL),), root * root * inverse))
            stores.append((t, (pl.ds(base, TALL),), q[pl.ds(here, TALL)] * inverse))
            if n == 0:
                stores.append((diag, (level,), d[ROWS:MID]))
        return stores

    over_layers(first, 8)

    lead = ROWS // 2

    def second(level):
        base = pl.multiple_of((level + 1) * TALL, 8) + lead
        sums = around(t0_c, t0_h, base, TALL, MID)
        to = (pl.ds(pl.multiple_of((level + 1) * MID, 8), MID),)
        return [
            (t_c[0], to, g_c[pl.ds(base - TALL, MID)] * sums[0]),
            (t_h[0], to, g_h[pl.ds(base - TALL, MID)] * sums[1]),
        ]

    over_layers(second, 16)

    for j in range(1, ITERS):
        def later(level, j=j):
            base = pl.multiple_of((level + 1) * MID, 8)
            from_g = pl.multiple_of(level * TALL, 8) + lead
            sums = around(t_c[j - 1], t_h[j - 1], base, MID, MID)
            if j == 1:
                start = pl.multiple_of((level + 1) * TALL, 8) + lead
                before = t0_c[pl.ds(start, MID)], t0_h[pl.ds(start, MID)]
            else:
                before = t_c[j - 2][pl.ds(base, MID)], t_h[j - 2][pl.ds(base, MID)]
            to = (pl.ds(base, MID),)
            return [
                (t_c[j], to, 2.0 * g_c[pl.ds(from_g, MID)] * sums[0] - before[0]),
                (t_h[j], to, 2.0 * g_h[pl.ds(from_g, MID)] * sums[1] - before[1]),
            ]

        over_layers(later, 16)

    def last(level):
        base = pl.multiple_of((level + 1) * MID, 8) + lead
        tall = pl.multiple_of(level * TALL, 8) + ROWS
        sums = around(t_c[ITERS - 1], t_h[ITERS - 1], base, MID, ROWS)
        t = [t0_c[pl.ds(tall + TALL, ROWS)]] + [t_c[j][pl.ds(base, ROWS)] for j in range(ITERS)]
        t.append(2.0 * g_c[pl.ds(tall, ROWS)] * sums[0] - t[ITERS - 1])
        root = s_c[pl.ds(tall + TALL, ROWS)]
        inv = jnp.where(root > 0.0, 1.0 / root, 0.0)
        ratio = diag[level] * inv
        weight = ratio * inv
        stores = [(basis, (j, level), t[j]) for j in range(BASIS)]
        stores += [(inv_root, (level,), inv), (scale, (level,), ratio)]
        terms = []
        for j in range(ITERS):
            weighted = weight * t[j]
            terms += [weighted * t[j], weighted * t[j + 1]]
        return stores, terms

    def last_block(k, totals):
        stores = []
        for m in range(8):
            more, terms = last(k * 8 + m)
            stores += more
            totals = tuple(a + b for a, b in zip(totals, terms))
        put(stores)
        return totals

    zero = jnp.zeros((ROWS, LANES), jnp.float32)
    totals = lax.fori_loop(0, LAYERS // 8, last_block, (zero,) * (2 * ITERS))
    column = lane_index(1)
    row = jnp.zeros((1, LANES), jnp.float32)
    for n, total in enumerate(totals):
        row = jnp.where(column == n, jnp.sum(jnp.sum(total, axis=0, keepdims=True), axis=1, keepdims=True), row)
    moments[...] = row


def added(a, b, factor):
    out = []
    for i in range(max(len(a), len(b))):
        left = a[i] if i < len(a) else None
        right = b[i] if i < len(b) else None
        if right is not None:
            right = factor * right
        out.append(right if left is None else left if right is None else left + right)
    return out


def shifted(a):
    out = [None] * (len(a) + 1)

    def put(i, value):
        out[i] = value if out[i] is None else out[i] + value

    for i, value in enumerate(a):
        if i == 0:
            put(1, value)
        else:
            put(i + 1, 0.5 * value)
            put(i - 1, 0.5 * value)
    return out


def form(a, b, gram):
    total = None
    for i, left in enumerate(a):
        inner = None
        for j, right in enumerate(b):
            if right is None:
                continue
            term = right * gram(i, j)
            inner = term if inner is None else inner + term
        inner = left * inner
        total = inner if total is None else total + inner
    return total


def recursion(moments):
    half = [0.5 * m for m in moments]

    def gram(i, j):
        return moments[i] if j == 0 else moments[j] if i == 0 else half[i + j] + half[abs(i - j)]

    one = jnp.ones_like(moments[0])
    precond, direction, head = [one], [], []
    gamma_old = alpha_old = None
    for step in range(ITERS):
        gamma = form(precond, precond, gram)
        delta = gamma - form(precond, shifted(precond), gram)
        if step == 0:
            direction = precond
            alpha = gamma / delta
        else:
            beta = gamma / gamma_old
            alpha = gamma / (delta - beta * gamma / alpha_old)
            direction = added(precond, direction, beta)
        head = added(head, direction, alpha)
        moved = added(direction, shifted(direction), -1.0)
        precond = added(precond, moved, -alpha)
        gamma_old, alpha_old = gamma, alpha
    return head, precond, added(precond, shifted(precond), -1.0)


def combine_kernel(moments, basis, inv_root, scale, head_field, residual, applied):
    row = jnp.sum(moments[...], axis=0)
    column = lane_index(1)
    raw = []
    for n in range(2 * ITERS):
        value = jnp.sum(jnp.where(column == n, row, 0.0), axis=1, keepdims=True)
        raw.append(jnp.broadcast_to(value, (ROWS, LANES)))
    full = raw[:2]
    for n in range(2, 2 * ITERS):
        full.append(2.0 * raw[n] - raw[n % 2])
    coefficients = recursion(full)

    def write(level, _):
        t = [basis[j, level] for j in range(BASIS)]
        outs = []
        for weights in coefficients:
            total = weights[0] * t[0]
            for j in range(1, len(weights)):
                total = total + weights[j] * t[j]
            outs.append(total)
        factor = scale[level]
        head_field[level] = inv_root[level] * outs[0]
        residual[level] = factor * outs[1]
        applied[level] = factor * outs[2]
        return 0

    lax.fori_loop(0, LAYERS, write, 0)


def f32(*shape):
    return jax.ShapeDtypeStruct(shape, jnp.float32)


def scratch(*shape):
    return pltpu.VMEM(shape, jnp.float32)


def call(kernel, outs, scratches=()):
    whole = pl.BlockSpec(memory_space=pltpu.VMEM)
    return pl.pallas_call(
        kernel,
        out_shape=outs,
        out_specs=[whole] * len(outs),
        scratch_shapes=list(scratches),
        compiler_params=pltpu.CompilerParams(vmem_limit_bytes=32 * 1024 * 1024),
    )


def shift_both(low_going, high_going, axis):
    count = lax.axis_size(axis)
    up = [(i, i + 1) for i in range(count - 1)]
    down = [(target, source) for source, target in up]
    return lax.ppermute(high_going, axis, up), lax.ppermute(low_going, axis, down)


def spread_sum(row, axes):
    count = lax.axis_size(axes)
    got = lax.all_to_all(jnp.broadcast_to(row[None], (count,) + row.shape), axes, 0, 0, tiled=True)
    return got


def pack(recharge, conduct, top_layer, fixed_head):
    shapes = (f32(PLANES + 2 * PACKED, ROWS, LANES), f32(PACKED, ROWS, LANES), f32(PACKED, ROWS, LANES))
    return call(pack_kernel, shapes)(recharge, conduct, top_layer, fixed_head)


def make_basis(fields, low, high):
    field = f32(LAYERS, ROWS, LANES)
    tall, mid = (LAYERS + 2) * TALL, (LAYERS + 2) * MID
    plain = LAYERS * TALL
    scratches = [scratch(tall, LANES)] * 2 + [scratch(plain, LANES)] * 2 + [scratch(TALL, LANES)] * 2
    scratches += [scratch(plain, LANES)] * 2 + [scratch(LAYERS, ROWS, LANES)] + [scratch(tall, LANES)] * 2
    scratches += [scratch(mid, LANES)] * (2 * ITERS)
    outs = (f32(BASIS, LAYERS, ROWS, LANES), field, field, f32(1, LANES))
    return call(basis_kernel, outs, scratches)(fields, low, high)


def combine(moments, basis, inv_root, scale):
    return call(combine_kernel, (f32(LAYERS, ROWS, LANES),) * 3)(moments, basis, inv_root, scale)


def local(recharge, conduct, top_layer, fixed_head):
    fields, low_edge, high_edge = pack(recharge, conduct, top_layer, fixed_head)
    from_low, from_high = shift_both(low_edge, high_edge, "y")
    fields = lax.dynamic_update_slice(fields, jnp.concatenate([from_high, from_low], axis=0), (PLANES, 0, 0))
    low, high = shift_both(fields, fields, GX)
    basis, inv_root, scale, moments = make_basis(fields, low, high)
    moments = jnp.sum(spread_sum(moments, ("z", "c")), axis=0)
    moments = spread_sum(moments, ("x", "y"))
    return combine(moments, basis, inv_root, scale)


def solution(mesh):
    grid = Mesh(mesh.devices.reshape(12, 4, 2, 8), ("z", "x", "c", "y"))
    field, plane = P(None, GX, "y"), P(GX, "y")
    return jax.shard_map(
        local, mesh=grid, in_specs=(field, field, plane, plane), out_specs=(field, field, field), check_vma=False
    )
```

```python
import jax
import jax.numpy as jnp
from jax import lax
from jax.experimental import pallas as pl
from jax.experimental.pallas import tpu as pltpu
from jax.sharding import Mesh, PartitionSpec as P

ITERS = 4
LAYERS = 48
ROWS = 8
LANES = 128
BASIS = ITERS + 2
DEPTH = BASIS
SPAN = ROWS + 2 * DEPTH
WIDTH = 2 * LAYERS + 8
UNITS = WIDTH // 8
SLOTS = 16
STRIDE = LAYERS + 8
FIRST = SPAN - 2
LEAD = (FIRST - ROWS) // 2

store_term = 0.1
boundary_term = 4.0
vertical_ratio = 0.3

GX = ("z", "x", "c")


def lane_index(rows):
    return lax.broadcasted_iota(jnp.int32, (rows, LANES), 1)


def padded(row):
    return 8 + row * STRIDE


def zero_padding(ref, rows):
    blank = jnp.zeros((8, LANES), jnp.float32)
    for row in range(rows + 1):
        ref[pl.ds(row * STRIDE, 8)] = blank


def rows_in_blocks(count, unroll, step):
    def block(k, _):
        stores = []
        for m in range(unroll):
            stores += step(k * unroll + m)
        for ref, where, value in stores:
            ref[where] = value
        return 0

    lax.fori_loop(0, count // unroll, block, 0)


def prepare_kernel(recharge, conduct, top_layer, fixed_head, main, part, r_buf, c_buf, t_buf, f_buf, sems):
    pairs = ((conduct, c_buf), (top_layer, t_buf), (recharge, r_buf), (fixed_head, f_buf))
    copies = [pltpu.make_async_copy(a, b, sems.at[n]) for n, (a, b) in enumerate(pairs)]
    for copy in copies:
        copy.start()
    for copy in copies:
        copy.wait()
    core = lax.axis_index("c")
    level = lax.broadcasted_iota(jnp.int32, (LAYERS, LANES), 0)
    for row in range(ROWS):
        conductivity = c_buf[pl.ds(row, LAYERS, stride=ROWS)]
        root = jnp.where(level >= t_buf[row:row + 1], jnp.sqrt(conductivity), 0.0)
        main[row, :LAYERS] = root
        main[row, LAYERS:2 * LAYERS] = root * r_buf[pl.ds(row, LAYERS, stride=ROWS)]
        main[row, 2 * LAYERS:] = jnp.broadcast_to(f_buf[row:row + 1].astype(jnp.float32), (8, LANES))
    for row in range(DEPTH):
        part[row] = main[(ROWS - DEPTH) * core + row]


def span_rows(both, far):
    core = lax.axis_index("c")
    near = [(both, (ROWS - DEPTH) * core + n, DEPTH * (1 - core) + n) for n in range(ROWS + DEPTH)]
    return near + [(far, n, (ROWS + DEPTH) * core + n) for n in range(DEPTH)]


def edges_kernel(both, far, low_edge, high_edge):
    slot = lane_index(ROWS) // 8
    for ref, source, row in span_rows(both, far):
        low = jnp.zeros((8, LANES), jnp.float32)
        high = jnp.zeros((8, LANES), jnp.float32)
        for u in range(UNITS):
            turned = ref[source, 8 * u:8 * u + 8]
            if u:
                turned = pltpu.roll(turned, 8 * u, 1)
            low = jnp.where(slot == u, turned, low)
            high = jnp.where(slot == (u - 1) % SLOTS, turned, high)
        low_edge[row] = low
        high_edge[row] = high


def assemble_kernel(both, far, root, source, fixed, near, across):
    zero_padding(root, SPAN)
    for ref, at, row in span_rows(both, far):
        root[pl.ds(pl.multiple_of(padded(row), 8), LAYERS)] = ref[at, :LAYERS]
        source[row] = ref[at, LAYERS:2 * LAYERS]
        fixed[row] = boundary_term * ref[at, 2 * LAYERS:]
    lane = lane_index(LAYERS)
    last, first = lane == LANES - 1, lane == 0

    def sums(i):
        base = pl.multiple_of(padded(i + 1), 8)
        center = root[pl.ds(base, LAYERS)]
        up, down = pltpu.roll(center, LANES - 1, 1), pltpu.roll(center, 1, 1)
        total = jnp.where(last, 0.0, up) + jnp.where(first, 0.0, down) + straight(root, base)
        return [(near, i, total), (across, i, jnp.where(last, up, jnp.where(first, down, 0.0)))]

    rows_in_blocks(FIRST, 3, sums)


def straight(ref, base):
    rows = ref[pl.ds(base - STRIDE, LAYERS)] + ref[pl.ds(base + STRIDE, LAYERS)]
    return rows + vertical_ratio * (ref[pl.ds(base - 1, LAYERS)] + ref[pl.ds(base + 1, LAYERS)])


def basis_kernel(root_c, source_c, fixed_c, near, across, from_low, from_high, basis, inv_root, scale, moments,
                 root_h, source_h, fixed_h, g_c, g_h, diag, *fields):
    t_c, t_h = fields[:ITERS + 1], fields[ITERS + 1:]
    lane = lane_index(8)
    rim = (lane < 8) | (lane >= LANES - 8)
    zero_padding(root_h, SPAN)
    for j in range(ITERS + 1):
        zero_padding(t_c[j], FIRST - 2 * j)
        zero_padding(t_h[j], FIRST - 2 * j)

    def unpack(row):
        high, low = from_high[row], from_low[row]
        start = pl.multiple_of(padded(row), 8)
        stores = []
        for u in range(UNITS):
            tile = jnp.where(lane // 8 == u, high, low)
            if u:
                tile = pltpu.roll(tile, LANES - 8 * u, 1)
            tile = jnp.where(rim, tile, 0.0)
            if u < LAYERS // 8:
                stores.append((root_h, pl.ds(start + 8 * u, 8), tile))
            elif u < 2 * LAYERS // 8:
                stores.append((source_h, (row, pl.ds(8 * u - LAYERS, 8)), tile))
            else:
                stores.append((fixed_h, row, boundary_term * tile))
        return stores

    rows_in_blocks(SPAN, 5, unpack)

    wide = lane_index(LAYERS)
    last, first = wide == LANES - 1, wide == 0

    def start(i):
        base = pl.multiple_of(padded(i + 1), 8)
        to = pl.ds(pl.multiple_of(padded(i), 8), LAYERS)
        halo = root_h[pl.ds(base, LAYERS)]
        up, down = pltpu.roll(halo, LANES - 1, 1), pltpu.roll(halo, 1, 1)
        c_sum = near[i] + jnp.where(last, up, jnp.where(first, down, 0.0))
        h_sum = jnp.where(last, 0.0, up) + jnp.where(first, 0.0, down) + across[i] + straight(root_h, base)
        stores = []
        parts = (
            (root_c, c_sum, source_c, fixed_c, g_c, t_c[0], diag),
            (root_h, h_sum, source_h, fixed_h, g_h, t_h[0], None),
        )
        for roots, total, source, fixed, g, t, keep in parts:
            root = roots[pl.ds(base, LAYERS)]
            above = roots[pl.ds(base - 1, LAYERS)]
            head = jnp.where(above > 0.0, 0.0, fixed[i + 1, :1])
            d = jnp.where(root > 0.0, root * total + (store_term + head), 1.0)
            inverse = 1.0 / d
            stores.append((g, i, root * root * inverse))
            stores.append((t, to, source[i + 1] * inverse))
            if keep is not None:
                stores.append((keep, i, d))
        return stores

    rows_in_blocks(FIRST, 3, start)

    def sums(c_ref, h_ref, base):
        center, halo = c_ref[pl.ds(base, LAYERS)], h_ref[pl.ds(base, LAYERS)]
        c_up, h_up = pltpu.roll(center, LANES - 1, 1), pltpu.roll(halo, LANES - 1, 1)
        c_down, h_down = pltpu.roll(center, 1, 1), pltpu.roll(halo, 1, 1)
        c_sum = jnp.where(last, h_up, c_up) + jnp.where(first, h_down, c_down) + straight(c_ref, base)

        def halo_sum():
            return jnp.where(last, c_up, h_up) + jnp.where(first, c_down, h_down) + straight(h_ref, base)

        return c_sum, halo_sum

    def field(ref, row):
        return ref[pl.ds(pl.multiple_of(padded(row), 8), LAYERS)]

    for j, unroll in zip(range(1, ITERS + 1), (4, 7, 6, 5)):
        def step(i, j=j):
            c_sum, halo_sum = sums(t_c[j - 1], t_h[j - 1], pl.multiple_of(padded(i + 1), 8))
            out = [g_c[i + j] * c_sum, g_h[i + j] * halo_sum()]
            if j > 1:
                out = [2.0 * a - field(t[j - 2], i + 2) for a, t in zip(out, (t_c, t_h))]
            to = pl.ds(pl.multiple_of(padded(i), 8), LAYERS)
            return [(t_c[j], to, out[0]), (t_h[j], to, out[1])]

        rows_in_blocks(FIRST - 2 * j, unroll, step)

    unroll = 2

    def finish(k, totals):
        stores = []
        for m in range(unroll):
            i = k * unroll + m
            c_sum, _ = sums(t_c[ITERS], t_h[ITERS], pl.multiple_of(padded(i + 1), 8))
            t = [field(t_c[j], i + LEAD - j) for j in range(ITERS + 1)]
            t.append(2.0 * g_c[i + LEAD] * c_sum - t[ITERS - 1])
            stores += [(basis, (j, i), t[j]) for j in range(BASIS)]
            root = field(root_c, i + DEPTH)
            inv = jnp.where(root > 0.0, 1.0 / root, 0.0)
            ratio = diag[i + LEAD] * inv
            stores += [(inv_root, i, inv), (scale, i, ratio)]
            weight = ratio * inv
            new = []
            for j in range(ITERS):
                weighted = weight * t[j]
                new += [weighted * t[j], weighted * t[j + 1]]
            totals = tuple(a + b for a, b in zip(totals, new))
        for ref, where, value in stores:
            ref[where] = value
        return totals

    zero = jnp.zeros((LAYERS, LANES), jnp.float32)
    totals = lax.fori_loop(0, ROWS // unroll, finish, (zero,) * (2 * ITERS))
    column = lane_index(1)
    row = jnp.zeros((1, LANES), jnp.float32)
    for n, total in enumerate(totals):
        row = jnp.where(column == n, jnp.sum(jnp.sum(total, axis=0, keepdims=True), axis=1, keepdims=True), row)
    moments[...] = row


def added(a, b, factor):
    out = []
    for i in range(max(len(a), len(b))):
        left = a[i] if i < len(a) else None
        right = b[i] if i < len(b) else None
        if right is not None:
            right = factor * right
        out.append(right if left is None else left if right is None else left + right)
    return out


def shifted(a):
    out = [None] * (len(a) + 1)

    def put(i, value):
        out[i] = value if out[i] is None else out[i] + value

    for i, value in enumerate(a):
        if i == 0:
            put(1, value)
        else:
            put(i + 1, 0.5 * value)
            put(i - 1, 0.5 * value)
    return out


def form(a, b, gram):
    total = None
    for i, left in enumerate(a):
        inner = None
        for j, right in enumerate(b):
            if right is None:
                continue
            term = right * gram(i, j)
            inner = term if inner is None else inner + term
        inner = left * inner
        total = inner if total is None else total + inner
    return total


def recursion(moments):
    half = [0.5 * m for m in moments]

    def gram(i, j):
        return moments[i] if j == 0 else moments[j] if i == 0 else half[i + j] + half[abs(i - j)]

    one = jnp.ones_like(moments[0])
    precond, direction, head = [one], [], []
    gamma_old = alpha_old = None
    for step in range(ITERS):
        gamma = form(precond, precond, gram)
        delta = gamma - form(precond, shifted(precond), gram)
        if step == 0:
            direction = precond
            alpha = gamma / delta
        else:
            beta = gamma / gamma_old
            alpha = gamma / (delta - beta * gamma / alpha_old)
            direction = added(precond, direction, beta)
        head = added(head, direction, alpha)
        moved = added(direction, shifted(direction), -1.0)
        precond = added(precond, moved, -alpha)
        gamma_old, alpha_old = gamma, alpha
    return head, precond, added(precond, shifted(precond), -1.0)


def combine_kernel(moments, basis, inv_root, scale, head_field, residual, applied, h_buf, r_buf, a_buf, sems):
    row = jnp.sum(moments[...], axis=0)
    column = lane_index(1)
    raw = []
    for n in range(2 * ITERS):
        value = jnp.sum(jnp.where(column == n, row, 0.0), axis=1, keepdims=True)
        raw.append(jnp.broadcast_to(value, (8, LANES)))
    full = raw[:2]
    for n in range(2, 2 * ITERS):
        full.append(2.0 * raw[n] - raw[n % 2])
    targets = ((h_buf, head_field, inv_root), (r_buf, residual, scale), (a_buf, applied, scale))
    copies = []
    for n, (weights, (buf, out, factor)) in enumerate(zip(recursion(full), targets)):
        weights = [jnp.concatenate([w] * (LAYERS // 8), axis=0) for w in weights]
        for row in range(ROWS):
            total = weights[0] * basis[0, row]
            for j in range(1, len(weights)):
                total = total + weights[j] * basis[j, row]
            buf[pl.ds(row, LAYERS, stride=ROWS)] = factor[row] * total
        copies.append(pltpu.make_async_copy(buf, out, sems.at[n]))
        copies[-1].start()
    for copy in copies:
        copy.wait()


def f32(*shape):
    return jax.ShapeDtypeStruct(shape, jnp.float32)


def scratch(*shape):
    return pltpu.VMEM(shape, jnp.float32)


VMEM = pl.BlockSpec(memory_space=pltpu.VMEM)
HBM = pl.BlockSpec(memory_space=pltpu.HBM)


def call(kernel, outs, scratches=(), ins=VMEM, out=VMEM):
    def run(*args):
        return pl.pallas_call(
            kernel,
            out_shape=outs,
            in_specs=[ins] * len(args),
            out_specs=[out] * len(outs),
            scratch_shapes=list(scratches),
            compiler_params=pltpu.CompilerParams(vmem_limit_bytes=32 * 1024 * 1024),
        )(*args)

    return run


def prepare(recharge, conduct, top_layer, fixed_head):
    flat = (LAYERS * ROWS, LANES)
    plane = pltpu.VMEM((ROWS, LANES), jnp.int32)
    args = (recharge.reshape(flat), conduct.reshape(flat), top_layer, fixed_head)
    return call(
        prepare_kernel,
        (f32(ROWS, WIDTH, LANES), f32(DEPTH, WIDTH, LANES)),
        [scratch(*flat), scratch(*flat), plane, plane, pltpu.SemaphoreType.DMA((4,))],
        ins=HBM,
    )(*[pltpu.with_memory_space_constraint(a, pltpu.HBM) for a in args])


def edges(both, far):
    return call(edges_kernel, (f32(SPAN, 8, LANES),) * 2)(both, far)


def assemble(both, far):
    field = f32(FIRST, LAYERS, LANES)
    outs = (f32(padded(SPAN), LANES), f32(SPAN, LAYERS, LANES), f32(SPAN, 8, LANES), field, field)
    return call(assemble_kernel, outs)(both, far)


def make_basis(parts, from_low, from_high):
    field = f32(ROWS, LAYERS, LANES)
    layers = scratch(FIRST, LAYERS, LANES)
    scratches = [scratch(padded(SPAN), LANES), scratch(SPAN, LAYERS, LANES), scratch(SPAN, 8, LANES)]
    scratches += [layers] * 3 + [scratch(padded(FIRST - 2 * j), LANES) for j in range(ITERS + 1)] * 2
    outs = (f32(BASIS, ROWS, LAYERS, LANES), field, field, f32(1, LANES))
    return call(basis_kernel, outs, scratches)(*parts, from_low, from_high)


def combine(moments, basis, inv_root, scale):
    flat = (LAYERS * ROWS, LANES)
    outs = call(
        combine_kernel,
        (f32(*flat),) * 3,
        [scratch(*flat)] * 3 + [pltpu.SemaphoreType.DMA((3,))],
        out=HBM,
    )(moments, basis, inv_root, scale)
    return tuple(out.reshape(LAYERS, ROWS, LANES) for out in outs)


def shift_both(low_going, high_going, axis):
    count = lax.axis_size(axis)
    up = [(i, i + 1) for i in range(count - 1)]
    down = [(target, source) for source, target in up]
    return lax.ppermute(high_going, axis, up), lax.ppermute(low_going, axis, down)


def between_chips(array):
    count = lax.axis_size(GX)
    pairs = []
    for i in range(1, count - 1, 2):
        pairs += [(i, i + 1), (i + 1, i)]
    return lax.ppermute(array, GX, pairs)


def spread_sum(row, axes):
    count = lax.axis_size(axes)
    return lax.all_to_all(jnp.broadcast_to(row[None], (count,) + row.shape), axes, 0, 0, tiled=True)


def local(recharge, conduct, top_layer, fixed_head):
    main, part = prepare(recharge, conduct, top_layer, fixed_head)
    far = between_chips(part)
    both = lax.all_gather(main, "c", axis=0, tiled=True)
    low_edge, high_edge = edges(both, far)
    from_low, from_high = shift_both(low_edge, high_edge, "y")
    parts = assemble(both, far)
    basis, inv_root, scale, moments = make_basis(parts, from_low, from_high)
    moments = jnp.sum(spread_sum(moments, ("z", "c")), axis=0)
    moments = spread_sum(moments, ("x", "y"))
    return combine(moments, basis, inv_root, scale)


def solution(mesh):
    grid = Mesh(mesh.devices.reshape(12, 4, 2, 8), ("z", "x", "c", "y"))
    field, plane = P(None, GX, "y"), P(GX, "y")
    return jax.shard_map(
        local, mesh=grid, in_specs=(field, field, plane, plane), out_specs=(field, field, field), check_vma=False
    )
```

```python
import jax
import jax.numpy as jnp
from jax import lax
from jax.experimental import pallas as pl
from jax.experimental.pallas import tpu as pltpu
from jax.sharding import Mesh, PartitionSpec as P

ITERS = 4
LAYERS = 48
ROWS = 8
LANES = 128
BASIS = ITERS + 2
DEPTH = BASIS
SPAN = ROWS + 2 * DEPTH
WIDTH = 2 * LAYERS + 8
TILES = LAYERS // 8
FIRST = SPAN - 2
LEAD = (FIRST - ROWS) // 2

EDGE = 7
SIDE = 3 * EDGE
PAIR = 2 * SIDE
FOLD = 3
STRIPS = 7
DENSE = 3 * STRIPS
MERGE = 8

store_term = 0.1
boundary_term = 4.0
vertical_ratio = 0.3

GX = ("z", "x", "c")


def lane_index(rows):
    return lax.broadcasted_iota(jnp.int32, (rows, LANES), 1)


def turn(tile, lanes):
    lanes %= LANES
    return pltpu.roll(tile, lanes, 1) if lanes else tile


def between(lane, low, high):
    return (lane >= low) & (lane < high)


def layer_above(row):
    sublane = lax.broadcasted_iota(jnp.int32, (8, LANES), 0)
    edge = jnp.where(sublane == 0, 0.0, pltpu.roll(row[LAYERS - 8:], 1, 0))
    return jnp.concatenate([edge, row[:LAYERS - 8]], axis=0)


def layer_below(row):
    sublane = lax.broadcasted_iota(jnp.int32, (8, LANES), 0)
    edge = jnp.where(sublane == 7, 0.0, pltpu.roll(row[:8], 7, 0))
    return jnp.concatenate([row[8:], edge], axis=0)


def neighbours(row, before, after):
    sides = turn(row, 1) + turn(row, -1) + before + after
    return sides + vertical_ratio * (layer_above(row) + layer_below(row))


def start_fields(root, source, fixed, total):
    head = jnp.where(layer_above(root) > 0.0, 0.0, boundary_term * fixed)
    diagonal = jnp.where(root > 0.0, root * total + (store_term + head), 1.0)
    inverse = 1.0 / diagonal
    return diagonal, root * root * inverse, source * inverse


def outer_factors(root, diagonal):
    inv = jnp.where(root > 0.0, 1.0 / root, 0.0)
    return inv, diagonal * inv


def products(weight, fields):
    out = []
    for j in range(ITERS):
        weighted = weight * fields[j]
        out += [weighted * fields[j], weighted * fields[j + 1]]
    return out


def as_row(totals):
    column = lane_index(1)
    row = jnp.zeros((1, LANES), jnp.float32)
    for n, total in enumerate(totals):
        row = jnp.where(column == n, jnp.sum(jnp.sum(total, axis=0, keepdims=True), axis=1, keepdims=True), row)
    return row


def rows_in_blocks(count, unroll, step):
    def block(k, _):
        stores = []
        for m in range(unroll):
            stores += step(k * unroll + m)
        for ref, where, value in stores:
            ref[where] = value
        return 0

    lax.fori_loop(0, count // unroll, block, 0)


def prepare_kernel(recharge, conduct, top_layer, fixed_head, main, part, r_buf, c_buf, t_buf, f_buf, sems):
    pairs = ((conduct, c_buf), (top_layer, t_buf), (recharge, r_buf), (fixed_head, f_buf))
    copies = [pltpu.make_async_copy(a, b, sems.at[n]) for n, (a, b) in enumerate(pairs)]
    for copy in copies:
        copy.start()
    for copy in copies:
        copy.wait()
    core = lax.axis_index("c")
    level = TILES * lax.broadcasted_iota(jnp.int32, (8, LANES), 0)
    for row in range(ROWS):
        top = t_buf[row:row + 1]
        for k in range(TILES):
            layers = pl.ds(k * ROWS + row, 8, stride=TILES * ROWS)
            root = jnp.where(level + k >= top, jnp.sqrt(c_buf[layers]), 0.0)
            main[row, 8 * k:8 * k + 8] = root
            main[row, LAYERS + 8 * k:LAYERS + 8 * k + 8] = root * r_buf[layers]
        main[row, 2 * LAYERS:] = jnp.broadcast_to(f_buf[row:row + 1].astype(jnp.float32), (8, LANES))
    for row in range(DEPTH):
        part[row] = main[(ROWS - DEPTH) * core + row]


def units(strip):
    for slot in range(FOLD):
        row = slot * STRIPS + strip
        if row < SPAN:
            for unit in range(2 * TILES + 1):
                group, place = divmod(unit, TILES)
                yield 3 * strip + group, place, slot, row, 8 * unit


def edges_kernel(both, far, span, low_edge, high_edge):
    core = lax.axis_index("c")
    for n in range(ROWS + DEPTH):
        span[DEPTH * (1 - core) + n] = both[(ROWS - DEPTH) * core + n]
    for n in range(DEPTH):
        span[(ROWS + DEPTH) * core + n] = far[n]
    lane = lane_index(8)
    for strip in range(STRIPS):
        low = {3 * strip + g: jnp.zeros((8, LANES), jnp.float32) for g in range(3)}
        high = dict(low)
        for dense, place, slot, row, at in units(strip):
            to = PAIR * slot + EDGE * place
            turned = turn(span[row, at:at + 8], to)
            low[dense] = jnp.where(between(lane, to, to + EDGE), turned, low[dense])
            to = (to - EDGE) % LANES
            high[dense] = jnp.where(between(lane, to, to + EDGE), turned, high[dense])
        for dense in low:
            low_edge[dense] = low[dense]
            high_edge[dense] = high[dense]


def own_kernel(span, basis, inv_root, scale, moments, strip_root, strip_source, strip_fixed, g, diag, *t):
    def start(i):
        row = i + 1
        root = span[row, :LAYERS]
        total = neighbours(root, span[row - 1, :LAYERS], span[row + 1, :LAYERS])
        fixed = span[row, 2 * LAYERS:2 * LAYERS + 1]
        d, g_row, t_row = start_fields(root, span[row, LAYERS:2 * LAYERS], fixed, total)
        return [(diag, i, d), (g, i, g_row), (t[0], i, t_row)]

    rows_in_blocks(FIRST, 3, start)

    for j, unroll in zip(range(1, ITERS + 1), (4, 7, 6, 5)):
        def step(i, j=j):
            new = g[i + j] * neighbours(t[j - 1][i + 1], t[j - 1][i], t[j - 1][i + 2])
            return [(t[j], i, new if j == 1 else 2.0 * new - t[j - 2][i + 2])]

        rows_in_blocks(FIRST - 2 * j, unroll, step)

    wide = lane_index(LAYERS)
    inner = between(wide, MERGE, LANES - MERGE)
    unroll = 2

    def finish(k, totals):
        stores = []
        for m in range(unroll):
            i = k * unroll + m
            fields = [t[j][i + LEAD - j] for j in range(ITERS + 1)]
            sums = neighbours(t[ITERS][i + 1], t[ITERS][i], t[ITERS][i + 2])
            fields.append(2.0 * g[i + LEAD] * sums - fields[ITERS - 1])
            inv, ratio = outer_factors(span[i + DEPTH, :LAYERS], diag[i + LEAD])
            stores += [(basis, (j, i), fields[j]) for j in range(BASIS)]
            stores += [(inv_root, i, inv), (scale, i, ratio)]
            new = products(jnp.where(inner, ratio * inv, 0.0), fields)
            totals = tuple(a + b for a, b in zip(totals, new))
        for ref, where, value in stores:
            ref[where] = value
        return totals

    zero = jnp.zeros((LAYERS, LANES), jnp.float32)
    moments[...] = as_row(lax.fori_loop(0, ROWS // unroll, finish, (zero,) * (2 * ITERS)))

    lane = lane_index(8)
    for strip in range(STRIPS):
        for unit in range(2 * TILES + 1):
            tile = jnp.zeros((8, LANES), jnp.float32)
            for slot in range(FOLD):
                row = slot * STRIPS + strip
                if row < SPAN:
                    source, base = span[row, 8 * unit:8 * unit + 8], PAIR * slot
                    low, high = turn(source, base + EDGE), turn(source, base + PAIR - EDGE)
                    tile = jnp.where(between(lane, base + EDGE, base + SIDE), low, tile)
                    tile = jnp.where(between(lane, base + SIDE, base + PAIR - EDGE), high, tile)
            if unit < TILES:
                strip_root[strip, 8 * unit:8 * unit + 8] = tile
            elif unit < 2 * TILES:
                strip_source[strip, 8 * unit - LAYERS:8 * unit - LAYERS + 8] = tile
            else:
                strip_fixed[strip] = tile


def strips_kernel(own_moments, own_root, own_source, own_fixed, from_low, from_high,
                  basis, inv_root, scale, moments, root, source, g):
    lane = lane_index(8)
    low_lanes = high_lanes = lane < 0
    for slot in range(FOLD):
        base = PAIR * slot
        low_lanes = low_lanes | between(lane, base, base + EDGE)
        high_lanes = high_lanes | between(lane, base + PAIR - EDGE, base + PAIR)

    def with_halo(own, dense, place):
        low = turn(from_low[dense], EDGE - EDGE * place)
        high = turn(from_high[dense], PAIR - EDGE - EDGE * place)
        return jnp.where(low_lanes, low, jnp.where(high_lanes, high, own))

    fixed = []
    for q in range(STRIPS):
        for k in range(TILES):
            tile = pl.ds(8 * k, 8)
            root[q, tile] = with_halo(own_root[q, tile], 3 * q, k)
            source[q, tile] = with_halo(own_source[q, tile], 3 * q + 1, k)
        fixed.append(with_halo(own_fixed[q], 3 * q + 2, 0)[:1])

    def sums(ref, at):
        rows = [ref[(*at, q)] for q in range(STRIPS)]
        before = [turn(rows[-1], PAIR)] + rows[:-1]
        after = rows[1:] + [turn(rows[0], -PAIR)]
        return [neighbours(*three) for three in zip(rows, before, after)]

    wide = lane_index(LAYERS)
    own_lanes = []
    for slot in range(2):
        base = PAIR * slot
        low = between(wide, base + EDGE, base + EDGE + MERGE)
        own_lanes.append(low | between(wide, base + PAIR - EDGE - MERGE, base + PAIR - EDGE))

    weights = []
    for q, total in enumerate(sums(root, ())):
        d, g[q], basis[0, q] = start_fields(root[q], source[q], fixed[q], total)
        inv, ratio = outer_factors(root[q], d)
        inv_root[q] = inv
        scale[q] = ratio
    for j in range(1, BASIS):
        for q, total in enumerate(sums(basis, (j - 1,))):
            new = g[q] * total
            basis[j, q] = new if j == 1 else 2.0 * new - basis[j - 2, q]

    totals = None
    for q in range(STRIPS):
        mine = own_lanes[1] | own_lanes[0] if q == DEPTH else own_lanes[1]
        new = products(jnp.where(mine, scale[q] * inv_root[q], 0.0), [basis[j, q] for j in range(ITERS + 1)])
        totals = new if totals is None else [a + b for a, b in zip(totals, new)]
    moments[...] = own_moments[...] + as_row(totals)


def added(a, b, factor):
    out = []
    for i in range(max(len(a), len(b))):
        left = a[i] if i < len(a) else None
        right = b[i] if i < len(b) else None
        if right is not None:
            right = factor * right
        out.append(right if left is None else left if right is None else left + right)
    return out


def shifted(a):
    out = [None] * (len(a) + 1)

    def put(i, value):
        out[i] = value if out[i] is None else out[i] + value

    for i, value in enumerate(a):
        if i == 0:
            put(1, value)
        else:
            put(i + 1, 0.5 * value)
            put(i - 1, 0.5 * value)
    return out


def form(a, b, gram):
    total = None
    for i, left in enumerate(a):
        inner = None
        for j, right in enumerate(b):
            if right is None:
                continue
            term = right * gram(i, j)
            inner = term if inner is None else inner + term
        inner = left * inner
        total = inner if total is None else total + inner
    return total


def recursion(moments):
    half = [0.5 * m for m in moments]

    def gram(i, j):
        return moments[i] if j == 0 else moments[j] if i == 0 else half[i + j] + half[abs(i - j)]

    one = jnp.ones_like(moments[0])
    precond, direction, head = [one], [], []
    gamma_old = alpha_old = None
    for step in range(ITERS):
        gamma = form(precond, precond, gram)
        delta = gamma - form(precond, shifted(precond), gram)
        if step == 0:
            direction = precond
            alpha = gamma / delta
        else:
            beta = gamma / gamma_old
            alpha = gamma / (delta - beta * gamma / alpha_old)
            direction = added(precond, direction, beta)
        head = added(head, direction, alpha)
        moved = added(direction, shifted(direction), -1.0)
        precond = added(precond, moved, -alpha)
        gamma_old, alpha_old = gamma, alpha
    return head, precond, added(precond, shifted(precond), -1.0)


def combine_kernel(moments, basis, inv_root, scale, strip_basis, strip_inv_root, strip_scale,
                   head_field, residual, applied, h_buf, r_buf, a_buf, sems):
    row = jnp.sum(moments[...], axis=0)
    column = lane_index(1)
    raw = []
    for n in range(2 * ITERS):
        value = jnp.sum(jnp.where(column == n, row, 0.0), axis=1, keepdims=True)
        raw.append(jnp.broadcast_to(value, (8, LANES)))
    full = raw[:2]
    for n in range(2, 2 * ITERS):
        full.append(2.0 * raw[n] - raw[n % 2])
    lane = lane_index(LAYERS)
    low, high = lane < MERGE, lane >= LANES - MERGE
    targets = (
        (h_buf, head_field, inv_root, strip_inv_root),
        (r_buf, residual, scale, strip_scale),
        (a_buf, applied, scale, strip_scale),
    )
    copies = []
    for n, (weights, (buf, out, factor, strip_factor)) in enumerate(zip(recursion(full), targets)):
        weights = [jnp.concatenate([w] * TILES, axis=0) for w in weights]

        def total(fields, factors, at):
            value = weights[0] * fields[0, at]
            for j in range(1, len(weights)):
                value = value + weights[j] * fields[j, at]
            return factors[at] * value

        strips = [total(strip_basis, strip_factor, q) for q in range(STRIPS)]
        for row in range(ROWS):
            slot, q = divmod(row + DEPTH, STRIPS)
            base = PAIR * slot
            value = total(basis, factor, row)
            value = jnp.where(low, turn(strips[q], -base - EDGE), value)
            value = jnp.where(high, turn(strips[q], LANES - (base + PAIR - EDGE)), value)
            for k in range(TILES):
                buf[pl.ds(k * ROWS + row, 8, stride=TILES * ROWS)] = value[8 * k:8 * k + 8]
        copies.append(pltpu.make_async_copy(buf, out, sems.at[n]))
        copies[-1].start()
    for copy in copies:
        copy.wait()


def f32(*shape):
    return jax.ShapeDtypeStruct(shape, jnp.float32)


def scratch(*shape):
    return pltpu.VMEM(shape, jnp.float32)


VMEM = pl.BlockSpec(memory_space=pltpu.VMEM)
HBM = pl.BlockSpec(memory_space=pltpu.HBM)


def call(kernel, outs, scratches=(), ins=VMEM, out=VMEM):
    def run(*args):
        return pl.pallas_call(
            kernel,
            out_shape=outs,
            in_specs=[ins] * len(args),
            out_specs=[out] * len(outs),
            scratch_shapes=list(scratches),
            compiler_params=pltpu.CompilerParams(vmem_limit_bytes=32 * 1024 * 1024),
        )(*args)

    return run


def prepare(recharge, conduct, top_layer, fixed_head):
    flat = (LAYERS * ROWS, LANES)
    plane = pltpu.VMEM((ROWS, LANES), jnp.int32)
    args = (recharge.reshape(flat), conduct.reshape(flat), top_layer, fixed_head)
    return call(
        prepare_kernel,
        (f32(ROWS, WIDTH, LANES), f32(DEPTH, WIDTH, LANES)),
        [scratch(*flat), scratch(*flat), plane, plane, pltpu.SemaphoreType.DMA((4,))],
        ins=HBM,
    )(*[pltpu.with_memory_space_constraint(a, pltpu.HBM) for a in args])


def edges(both, far):
    dense = f32(DENSE, 8, LANES)
    return call(edges_kernel, (f32(SPAN, WIDTH, LANES), dense, dense))(both, far)


def own_columns(span):
    field, strip = f32(ROWS, LAYERS, LANES), f32(STRIPS, LAYERS, LANES)
    outs = (f32(BASIS, ROWS, LAYERS, LANES), field, field, f32(1, LANES), strip, strip, f32(STRIPS, 8, LANES))
    scratches = [scratch(FIRST, LAYERS, LANES)] * 2
    scratches += [scratch(FIRST - 2 * j, LAYERS, LANES) for j in range(ITERS + 1)]
    return call(own_kernel, outs, scratches)(span)


def strip_columns(moments, own, from_low, from_high):
    field = f32(STRIPS, LAYERS, LANES)
    outs = (f32(BASIS, STRIPS, LAYERS, LANES), field, field, f32(1, LANES))
    return call(strips_kernel, outs, [scratch(STRIPS, LAYERS, LANES)] * 3)(moments, *own, from_low, from_high)


def combine(moments, own, strips):
    flat = (LAYERS * ROWS, LANES)
    outs = call(
        combine_kernel,
        (f32(*flat),) * 3,
        [scratch(*flat)] * 3 + [pltpu.SemaphoreType.DMA((3,))],
        out=HBM,
    )(moments, *own, *strips)
    return tuple(out.reshape(LAYERS, ROWS, LANES) for out in outs)


def shift_both(low_going, high_going, axis):
    count = lax.axis_size(axis)
    up = [(i, i + 1) for i in range(count - 1)]
    down = [(target, source) for source, target in up]
    return lax.ppermute(high_going, axis, up), lax.ppermute(low_going, axis, down)


def between_chips(array):
    count = lax.axis_size(GX)
    pairs = []
    for i in range(1, count - 1, 2):
        pairs += [(i, i + 1), (i + 1, i)]
    return lax.ppermute(array, GX, pairs)


def spread_sum(row, axes):
    count = lax.axis_size(axes)
    return lax.all_to_all(jnp.broadcast_to(row[None], (count,) + row.shape), axes, 0, 0, tiled=True)


def local(recharge, conduct, top_layer, fixed_head):
    main, part = prepare(recharge, conduct, top_layer, fixed_head)
    far = between_chips(part)
    both = lax.all_gather(main, "c", axis=0, tiled=True)
    span, low_edge, high_edge = edges(both, far)
    from_low, from_high = shift_both(low_edge, high_edge, "y")
    *own, own_moments, root, source, fixed = own_columns(span)
    *strips, moments = strip_columns(own_moments, (root, source, fixed), from_low, from_high)
    moments = jnp.sum(spread_sum(moments, ("z", "c")), axis=0)
    moments = spread_sum(moments, ("x", "y"))
    return combine(moments, own, strips)


def solution(mesh):
    grid = Mesh(mesh.devices.reshape(12, 4, 2, 8), ("z", "x", "c", "y"))
    field, plane = P(None, GX, "y"), P(GX, "y")
    return jax.shard_map(
        local, mesh=grid, in_specs=(field, field, plane, plane), out_specs=(field, field, field), check_vma=False
    )
```

```python
import jax
import jax.numpy as jnp
from jax import lax
from jax.experimental import pallas as pl
from jax.experimental.pallas import tpu as pltpu
from jax.sharding import Mesh, PartitionSpec as P

ITERS = 4
LAYERS = 48
ROWS = 8
LANES = 128
BASIS = ITERS + 2
DEPTH = BASIS
SPAN = ROWS + 2 * DEPTH
WIDTH = 2 * LAYERS + 8
TILES = LAYERS // 8
FIRST = SPAN - 2
LEAD = (FIRST - ROWS) // 2

EDGE = 7
SIDE = 3 * EDGE
PAIR = 2 * SIDE
FOLD = 3
STRIPS = 7
DENSE = 3 * STRIPS
MERGE = 8

store_term = 0.1
boundary_term = 4.0
vertical_ratio = 0.3

GX = ("z", "x", "c")


def lane_index(rows):
    return lax.broadcasted_iota(jnp.int32, (rows, LANES), 1)


def turn(tile, lanes):
    lanes %= LANES
    return pltpu.roll(tile, lanes, 1) if lanes else tile


def between(lane, low, high):
    return (lane >= low) & (lane < high)


def layer_above(row):
    sublane = lax.broadcasted_iota(jnp.int32, (8, LANES), 0)
    edge = jnp.where(sublane == 0, 0.0, pltpu.roll(row[LAYERS - 8:], 1, 0))
    return jnp.concatenate([edge, row[:LAYERS - 8]], axis=0)


def layer_below(row):
    sublane = lax.broadcasted_iota(jnp.int32, (8, LANES), 0)
    edge = jnp.where(sublane == 7, 0.0, pltpu.roll(row[:8], 7, 0))
    return jnp.concatenate([row[8:], edge], axis=0)


def neighbours(row, before, after):
    sides = turn(row, 1) + turn(row, -1) + before + after
    return sides + vertical_ratio * (layer_above(row) + layer_below(row))


def start_fields(root, source, fixed, total):
    head = jnp.where(layer_above(root) > 0.0, 0.0, boundary_term * fixed)
    diagonal = jnp.where(root > 0.0, root * total + (store_term + head), 1.0)
    inverse = 1.0 / diagonal
    return diagonal, root * root * inverse, source * inverse


def outer_factors(root, diagonal):
    inv = jnp.where(root > 0.0, 1.0 / root, 0.0)
    return inv, diagonal * inv


def products(weight, fields):
    out = []
    for j in range(ITERS):
        weighted = weight * fields[j]
        out += [weighted * fields[j], weighted * fields[j + 1]]
    return out


def as_row(totals):
    column = lane_index(1)
    row = jnp.zeros((1, LANES), jnp.float32)
    for n, total in enumerate(totals):
        row = jnp.where(column == n, jnp.sum(jnp.sum(total, axis=0, keepdims=True), axis=1, keepdims=True), row)
    return row


def rows_in_blocks(count, unroll, step):
    def block(k, _):
        stores = []
        for m in range(unroll):
            stores += step(k * unroll + m)
        for ref, where, value in stores:
            ref[where] = value
        return 0

    lax.fori_loop(0, count // unroll, block, 0)


def prepare_kernel(recharge, conduct, top_layer, fixed_head, main, part, r_buf, c_buf, t_buf, f_buf, sems):
    pairs = ((conduct, c_buf), (top_layer, t_buf), (recharge, r_buf), (fixed_head, f_buf))
    copies = [pltpu.make_async_copy(a, b, sems.at[n]) for n, (a, b) in enumerate(pairs)]
    for copy in copies:
        copy.start()
    for copy in copies:
        copy.wait()
    core = lax.axis_index("c")
    level = TILES * lax.broadcasted_iota(jnp.int32, (8, LANES), 0)
    for row in range(ROWS):
        top = t_buf[row:row + 1]
        for k in range(TILES):
            layers = pl.ds(k * ROWS + row, 8, stride=TILES * ROWS)
            root = jnp.where(level + k >= top, jnp.sqrt(c_buf[layers]), 0.0)
            main[row, 8 * k:8 * k + 8] = root
            main[row, LAYERS + 8 * k:LAYERS + 8 * k + 8] = root * r_buf[layers]
        main[row, 2 * LAYERS:] = jnp.broadcast_to(f_buf[row:row + 1].astype(jnp.float32), (8, LANES))
    for row in range(DEPTH):
        part[row] = main[(ROWS - DEPTH) * core + row]


def units(strip):
    for slot in range(FOLD):
        row = slot * STRIPS + strip
        if row < SPAN:
            for unit in range(2 * TILES + 1):
                group, place = divmod(unit, TILES)
                yield 3 * strip + group, place, slot, row, 8 * unit


def edges_kernel(both, far, span, low_edge, high_edge):
    core = lax.axis_index("c")
    for n in range(ROWS + DEPTH):
        span[DEPTH * (1 - core) + n] = both[(ROWS - DEPTH) * core + n]
    for n in range(DEPTH):
        span[(ROWS + DEPTH) * core + n] = far[n]
    lane = lane_index(8)
    for strip in range(STRIPS):
        low = {3 * strip + g: jnp.zeros((8, LANES), jnp.float32) for g in range(3)}
        high = dict(low)
        for dense, place, slot, row, at in units(strip):
            to = PAIR * slot + EDGE * place
            turned = turn(span[row, at:at + 8], to)
            low[dense] = jnp.where(between(lane, to, to + EDGE), turned, low[dense])
            to = (to - EDGE) % LANES
            high[dense] = jnp.where(between(lane, to, to + EDGE), turned, high[dense])
        for dense in low:
            low_edge[dense] = low[dense]
            high_edge[dense] = high[dense]


def own_kernel(span, basis, inv_root, scale, moments, strip_root, strip_source, strip_fixed, g, diag, *t):
    def start(i):
        row = i + 1
        root = span[row, :LAYERS]
        total = neighbours(root, span[row - 1, :LAYERS], span[row + 1, :LAYERS])
        fixed = span[row, 2 * LAYERS:2 * LAYERS + 1]
        d, g_row, t_row = start_fields(root, span[row, LAYERS:2 * LAYERS], fixed, total)
        return [(diag, i, d), (g, i, g_row), (t[0], i, t_row)]

    rows_in_blocks(FIRST, 3, start)

    for j, unroll in zip(range(1, ITERS + 1), (4, 7, 6, 5)):
        def step(i, j=j):
            new = g[i + j] * neighbours(t[j - 1][i + 1], t[j - 1][i], t[j - 1][i + 2])
            return [(t[j], i, new if j == 1 else 2.0 * new - t[j - 2][i + 2])]

        rows_in_blocks(FIRST - 2 * j, unroll, step)

    wide = lane_index(LAYERS)
    inner = between(wide, MERGE, LANES - MERGE)
    unroll = 2

    def finish(k, totals):
        stores = []
        for m in range(unroll):
            i = k * unroll + m
            fields = [t[j][i + LEAD - j] for j in range(ITERS + 1)]
            sums = neighbours(t[ITERS][i + 1], t[ITERS][i], t[ITERS][i + 2])
            fields.append(2.0 * g[i + LEAD] * sums - fields[ITERS - 1])
            inv, ratio = outer_factors(span[i + DEPTH, :LAYERS], diag[i + LEAD])
            stores += [(basis, (j, i), fields[j]) for j in range(BASIS)]
            stores += [(inv_root, i, inv), (scale, i, ratio)]
            new = products(jnp.where(inner, ratio * inv, 0.0), fields)
            totals = tuple(a + b for a, b in zip(totals, new))
        for ref, where, value in stores:
            ref[where] = value
        return totals

    zero = jnp.zeros((LAYERS, LANES), jnp.float32)
    moments[...] = as_row(lax.fori_loop(0, ROWS // unroll, finish, (zero,) * (2 * ITERS)))

    lane = lane_index(8)
    for strip in range(STRIPS):
        for unit in range(2 * TILES + 1):
            tile = jnp.zeros((8, LANES), jnp.float32)
            for slot in range(FOLD):
                row = slot * STRIPS + strip
                if row < SPAN:
                    source, base = span[row, 8 * unit:8 * unit + 8], PAIR * slot
                    low, high = turn(source, base + EDGE), turn(source, base + PAIR - EDGE)
                    tile = jnp.where(between(lane, base + EDGE, base + SIDE), low, tile)
                    tile = jnp.where(between(lane, base + SIDE, base + PAIR - EDGE), high, tile)
            if unit < TILES:
                strip_root[strip, 8 * unit:8 * unit + 8] = tile
            elif unit < 2 * TILES:
                strip_source[strip, 8 * unit - LAYERS:8 * unit - LAYERS + 8] = tile
            else:
                strip_fixed[strip] = tile


def strips_kernel(own_moments, own_root, own_source, own_fixed, from_low, from_high,
                  basis, inv_root, scale, moments, root, source, g):
    lane = lane_index(8)
    low_lanes = high_lanes = lane < 0
    for slot in range(FOLD):
        base = PAIR * slot
        low_lanes = low_lanes | between(lane, base, base + EDGE)
        high_lanes = high_lanes | between(lane, base + PAIR - EDGE, base + PAIR)

    def with_halo(own, dense, place):
        low = turn(from_low[dense], EDGE - EDGE * place)
        high = turn(from_high[dense], PAIR - EDGE - EDGE * place)
        return jnp.where(low_lanes, low, jnp.where(high_lanes, high, own))

    fixed = []
    for q in range(STRIPS):
        for k in range(TILES):
            tile = pl.ds(8 * k, 8)
            root[q, tile] = with_halo(own_root[q, tile], 3 * q, k)
            source[q, tile] = with_halo(own_source[q, tile], 3 * q + 1, k)
        fixed.append(with_halo(own_fixed[q], 3 * q + 2, 0)[:1])

    def sums(ref, at):
        rows = [ref[(*at, q)] for q in range(STRIPS)]
        before = [turn(rows[-1], PAIR)] + rows[:-1]
        after = rows[1:] + [turn(rows[0], -PAIR)]
        return [neighbours(*three) for three in zip(rows, before, after)]

    wide = lane_index(LAYERS)
    own_lanes = []
    for slot in range(2):
        base = PAIR * slot
        low = between(wide, base + EDGE, base + EDGE + MERGE)
        own_lanes.append(low | between(wide, base + PAIR - EDGE - MERGE, base + PAIR - EDGE))

    weights = []
    for q, total in enumerate(sums(root, ())):
        d, g[q], basis[0, q] = start_fields(root[q], source[q], fixed[q], total)
        inv, ratio = outer_factors(root[q], d)
        inv_root[q] = inv
        scale[q] = ratio
    for j in range(1, BASIS):
        for q, total in enumerate(sums(basis, (j - 1,))):
            new = g[q] * total
            basis[j, q] = new if j == 1 else 2.0 * new - basis[j - 2, q]

    totals = None
    for q in range(STRIPS):
        mine = own_lanes[1] | own_lanes[0] if q == DEPTH else own_lanes[1]
        new = products(jnp.where(mine, scale[q] * inv_root[q], 0.0), [basis[j, q] for j in range(ITERS + 1)])
        totals = new if totals is None else [a + b for a, b in zip(totals, new)]
    moments[...] = own_moments[...] + as_row(totals)


def added(a, b, factor):
    out = []
    for i in range(max(len(a), len(b))):
        left = a[i] if i < len(a) else None
        right = b[i] if i < len(b) else None
        if right is not None:
            right = factor * right
        out.append(right if left is None else left if right is None else left + right)
    return out


def shifted(a):
    out = [None] * (len(a) + 1)

    def put(i, value):
        out[i] = value if out[i] is None else out[i] + value

    for i, value in enumerate(a):
        if i == 0:
            put(1, value)
        else:
            put(i + 1, 0.5 * value)
            put(i - 1, 0.5 * value)
    return out


def form(a, b, gram):
    total = None
    for i, left in enumerate(a):
        inner = None
        for j, right in enumerate(b):
            if right is None:
                continue
            term = right * gram(i, j)
            inner = term if inner is None else inner + term
        inner = left * inner
        total = inner if total is None else total + inner
    return total


def recursion(moments):
    half = [0.5 * m for m in moments]

    def gram(i, j):
        return moments[i] if j == 0 else moments[j] if i == 0 else half[i + j] + half[abs(i - j)]

    one = jnp.ones_like(moments[0])
    precond, direction, head = [one], [], []
    gamma_old = alpha_old = None
    for step in range(ITERS):
        gamma = form(precond, precond, gram)
        delta = gamma - form(precond, shifted(precond), gram)
        if step == 0:
            direction = precond
            alpha = gamma / delta
        else:
            beta = gamma / gamma_old
            alpha = gamma / (delta - beta * gamma / alpha_old)
            direction = added(precond, direction, beta)
        head = added(head, direction, alpha)
        moved = added(direction, shifted(direction), -1.0)
        precond = added(precond, moved, -alpha)
        gamma_old, alpha_old = gamma, alpha
    return head, precond, added(precond, shifted(precond), -1.0)


def combine_kernel(moments, basis, inv_root, scale, strip_basis, strip_inv_root, strip_scale,
                   head_field, residual, applied, h_buf, r_buf, a_buf, sems):
    row = jnp.sum(moments[...], axis=0)
    column = lane_index(1)
    raw = []
    for n in range(2 * ITERS):
        value = jnp.sum(jnp.where(column == n, row, 0.0), axis=1, keepdims=True)
        raw.append(jnp.broadcast_to(value, (8, LANES)))
    full = raw[:2]
    for n in range(2, 2 * ITERS):
        full.append(2.0 * raw[n] - raw[n % 2])
    lane = lane_index(LAYERS)
    low, high = lane < MERGE, lane >= LANES - MERGE
    targets = (
        (h_buf, head_field, inv_root, strip_inv_root),
        (r_buf, residual, scale, strip_scale),
        (a_buf, applied, scale, strip_scale),
    )
    copies = []
    for n, (weights, (buf, out, factor, strip_factor)) in enumerate(zip(recursion(full), targets)):
        weights = [jnp.concatenate([w] * TILES, axis=0) for w in weights]

        def total(fields, factors, at):
            value = weights[0] * fields[0, at]
            for j in range(1, len(weights)):
                value = value + weights[j] * fields[j, at]
            return factors[at] * value

        strips = [total(strip_basis, strip_factor, q) for q in range(STRIPS)]
        for row in range(ROWS):
            slot, q = divmod(row + DEPTH, STRIPS)
            base = PAIR * slot
            value = total(basis, factor, row)
            value = jnp.where(low, turn(strips[q], -base - EDGE), value)
            value = jnp.where(high, turn(strips[q], LANES - (base + PAIR - EDGE)), value)
            for k in range(TILES):
                buf[pl.ds(k * ROWS + row, 8, stride=TILES * ROWS)] = value[8 * k:8 * k + 8]
        copies.append(pltpu.make_async_copy(buf, out, sems.at[n]))
        copies[-1].start()
    for copy in copies:
        copy.wait()


def f32(*shape):
    return jax.ShapeDtypeStruct(shape, jnp.float32)


def scratch(*shape):
    return pltpu.VMEM(shape, jnp.float32)


VMEM = pl.BlockSpec(memory_space=pltpu.VMEM)
HBM = pl.BlockSpec(memory_space=pltpu.HBM)


def call(kernel, outs, scratches=(), ins=VMEM, out=VMEM):
    def run(*args):
        return pl.pallas_call(
            kernel,
            out_shape=outs,
            in_specs=[ins] * len(args),
            out_specs=[out] * len(outs),
            scratch_shapes=list(scratches),
            compiler_params=pltpu.CompilerParams(vmem_limit_bytes=32 * 1024 * 1024),
        )(*args)

    return run


def prepare(recharge, conduct, top_layer, fixed_head):
    flat = (LAYERS * ROWS, LANES)
    plane = pltpu.VMEM((ROWS, LANES), jnp.int32)
    args = (recharge.reshape(flat), conduct.reshape(flat), top_layer, fixed_head)
    return call(
        prepare_kernel,
        (f32(ROWS, WIDTH, LANES), f32(DEPTH, WIDTH, LANES)),
        [scratch(*flat), scratch(*flat), plane, plane, pltpu.SemaphoreType.DMA((4,))],
        ins=HBM,
    )(*[pltpu.with_memory_space_constraint(a, pltpu.HBM) for a in args])


def edges(both, far):
    dense = f32(DENSE, 8, LANES)
    return call(edges_kernel, (f32(SPAN, WIDTH, LANES), dense, dense))(both, far)


def own_columns(span):
    field, strip = f32(ROWS, LAYERS, LANES), f32(STRIPS, LAYERS, LANES)
    outs = (f32(BASIS, ROWS, LAYERS, LANES), field, field, f32(1, LANES), strip, strip, f32(STRIPS, 8, LANES))
    scratches = [scratch(FIRST, LAYERS, LANES)] * 2
    scratches += [scratch(FIRST - 2 * j, LAYERS, LANES) for j in range(ITERS + 1)]
    return call(own_kernel, outs, scratches)(span)


def strip_columns(moments, own, from_low, from_high):
    field = f32(STRIPS, LAYERS, LANES)
    outs = (f32(BASIS, STRIPS, LAYERS, LANES), field, field, f32(1, LANES))
    return call(strips_kernel, outs, [scratch(STRIPS, LAYERS, LANES)] * 3)(moments, *own, from_low, from_high)


def combine(moments, own, strips):
    flat = (LAYERS * ROWS, LANES)
    outs = call(
        combine_kernel,
        (f32(*flat),) * 3,
        [scratch(*flat)] * 3 + [pltpu.SemaphoreType.DMA((3,))],
        out=HBM,
    )(moments, *own, *strips)
    return tuple(out.reshape(LAYERS, ROWS, LANES) for out in outs)


def shift_both(low_going, high_going, axis):
    count = lax.axis_size(axis)
    up = [(i, i + 1) for i in range(count - 1)]
    down = [(target, source) for source, target in up]
    return lax.ppermute(high_going, axis, up), lax.ppermute(low_going, axis, down)


def between_chips(array):
    count = lax.axis_size(GX)
    pairs = []
    for i in range(1, count - 1, 2):
        pairs += [(i, i + 1), (i + 1, i)]
    return lax.ppermute(array, GX, pairs)


def spread_sum(row, axes, leader):
    count = lax.axis_size(axes)
    group = [(leader + i) % count for i in range(count)]
    rows = jnp.broadcast_to(row[None], (count,) + row.shape)
    return lax.all_to_all(rows, axes, 0, 0, axis_index_groups=[group], tiled=True)


def local(recharge, conduct, top_layer, fixed_head):
    main, part = prepare(recharge, conduct, top_layer, fixed_head)
    far = between_chips(part)
    both = lax.all_gather(main, "c", axis=0, tiled=True)
    span, low_edge, high_edge = edges(both, far)
    from_low, from_high = shift_both(low_edge, high_edge, "y")
    *own, own_moments, root, source, fixed = own_columns(span)
    *strips, moments = strip_columns(own_moments, (root, source, fixed), from_low, from_high)
    moments = jnp.sum(spread_sum(moments, ("z", "c"), 8 * 2), axis=0)
    moments = spread_sum(moments, ("x", "y"), 3 * 8 + 4)
    return combine(moments, own, strips)


def solution(mesh):
    grid = Mesh(mesh.devices.reshape(12, 4, 2, 8), ("z", "x", "c", "y"))
    field, plane = P(None, GX, "y"), P(GX, "y")
    return jax.shard_map(
        local, mesh=grid, in_specs=(field, field, plane, plane), out_specs=(field, field, field), check_vma=False
    )
```

```python
import jax
import jax.numpy as jnp
from jax import lax
from jax.experimental import pallas as pl
from jax.experimental.pallas import tpu as pltpu
from jax.sharding import Mesh, PartitionSpec as P

ITERS = 4
LAYERS = 48
ROWS = 8
LANES = 128
BASIS = ITERS + 2
DEPTH = BASIS
SPAN = ROWS + 2 * DEPTH
WIDTH = 2 * LAYERS + 8
TILES = LAYERS // 8
FIRST = SPAN - 2
LEAD = (FIRST - ROWS) // 2

EDGE = 7
SIDE = 3 * EDGE
PAIR = 2 * SIDE
FOLD = 3
STRIPS = 7
DENSE = 2 * STRIPS + 1
FAR = (2 * DEPTH - 1) * LAYERS + 8
MERGE = 8

store_term = 0.1
boundary_term = 4.0
vertical_ratio = 0.3

GX = ("z", "x", "c")


def lane_index(rows):
    return lax.broadcasted_iota(jnp.int32, (rows, LANES), 1)


def turn(tile, lanes):
    lanes %= LANES
    return pltpu.roll(tile, lanes, 1) if lanes else tile


def between(lane, low, high):
    return (lane >= low) & (lane < high)


def layer_above(row):
    sublane = lax.broadcasted_iota(jnp.int32, (8, LANES), 0)
    edge = jnp.where(sublane == 0, 0.0, pltpu.roll(row[LAYERS - 8:], 1, 0))
    return jnp.concatenate([edge, row[:LAYERS - 8]], axis=0)


def layer_below(row):
    sublane = lax.broadcasted_iota(jnp.int32, (8, LANES), 0)
    edge = jnp.where(sublane == 7, 0.0, pltpu.roll(row[:8], 7, 0))
    return jnp.concatenate([row[8:], edge], axis=0)


def neighbours(row, before, after):
    sides = turn(row, 1) + turn(row, -1) + before + after
    return sides + vertical_ratio * (layer_above(row) + layer_below(row))


def start_fields(root, source, fixed, total):
    head = jnp.where(layer_above(root) > 0.0, 0.0, boundary_term * fixed)
    diagonal = jnp.where(root > 0.0, root * total + (store_term + head), 1.0)
    inverse = 1.0 / diagonal
    return diagonal, root * root * inverse, source * inverse


def outer_factors(root, diagonal):
    inv = jnp.where(root > 0.0, 1.0 / root, 0.0)
    return inv, diagonal * inv


def products(weight, fields):
    out = []
    for j in range(ITERS):
        weighted = weight * fields[j]
        out += [weighted * fields[j], weighted * fields[j + 1]]
    return out


def as_row(totals):
    column = lane_index(1)
    row = jnp.zeros((1, LANES), jnp.float32)
    for n, total in enumerate(totals):
        row = jnp.where(column == n, jnp.sum(jnp.sum(total, axis=0, keepdims=True), axis=1, keepdims=True), row)
    return row


def rows_in_blocks(count, unroll, step):
    def block(k, _):
        stores = []
        for m in range(unroll):
            stores += step(k * unroll + m)
        for ref, where, value in stores:
            ref[where] = value
        return 0

    lax.fori_loop(0, count // unroll, block, 0)


def prepare_kernel(recharge, conduct, top_layer, fixed_head, main, part, r_buf, c_buf, t_buf, f_buf, sems):
    pairs = ((conduct, c_buf), (top_layer, t_buf), (recharge, r_buf), (fixed_head, f_buf))
    copies = [pltpu.make_async_copy(a, b, sems.at[n]) for n, (a, b) in enumerate(pairs)]
    for copy in copies:
        copy.start()
    core = lax.axis_index("c")
    level = TILES * lax.broadcasted_iota(jnp.int32, (8, LANES), 0)
    tiles = [(row, k, pl.ds(k * ROWS + row, 8, stride=TILES * ROWS)) for row in range(ROWS) for k in range(TILES)]
    copies[0].wait()
    copies[1].wait()
    for row, k, layers in tiles:
        root = jnp.where(level + k >= t_buf[row:row + 1], jnp.sqrt(c_buf[layers]), 0.0)
        main[row, 8 * k:8 * k + 8] = root
    nearest = [jnp.where(core == 0, n, ROWS - 1 - n) for n in range(DEPTH)]
    for n, row in enumerate(nearest):
        part[n * LAYERS:(n + 1) * LAYERS] = main[row, :LAYERS]
    copies[2].wait()
    copies[3].wait()
    for row, k, layers in tiles:
        main[row, LAYERS + 8 * k:LAYERS + 8 * k + 8] = main[row, 8 * k:8 * k + 8] * r_buf[layers]
    for n, row in enumerate(nearest[:-1]):
        part[(DEPTH + n) * LAYERS:(DEPTH + n + 1) * LAYERS] = main[row, LAYERS:2 * LAYERS]
    fixed = f_buf[...].astype(jnp.float32)
    part[FAR - 8:] = fixed
    for row in range(ROWS):
        main[row, 2 * LAYERS:] = jnp.broadcast_to(fixed[row:row + 1], (8, LANES))


def units(strip):
    for slot in range(FOLD):
        row = slot * STRIPS + strip
        if row < SPAN:
            for unit in range(2 * TILES):
                group, place = divmod(unit, TILES)
                yield 2 * strip + group, place, slot, row, 8 * unit
            yield DENSE - 1, 0, slot, row, 2 * LAYERS


def edges_kernel(both, far, span, low_edge, high_edge):
    core = lax.axis_index("c")
    for n in range(ROWS + DEPTH):
        span[DEPTH * (1 - core) + n] = both[(ROWS - DEPTH) * core + n]
    for n in range(DEPTH):
        row = jnp.where(core == 0, DEPTH - 1 - n, ROWS + DEPTH + n)
        span[row, :LAYERS] = far[n * LAYERS:(n + 1) * LAYERS]
        if n < DEPTH - 1:
            span[row, LAYERS:2 * LAYERS] = far[(DEPTH + n) * LAYERS:(DEPTH + n + 1) * LAYERS]
        else:
            span[row, LAYERS:2 * LAYERS] = jnp.zeros((LAYERS, LANES), jnp.float32)
        fixed = far[pl.ds(FAR - 8 + jnp.where(core == 0, ROWS - 1 - n, n), 1)]
        span[row, 2 * LAYERS:] = jnp.broadcast_to(fixed, (8, LANES))
    lane = lane_index(8)
    sublane = lax.broadcasted_iota(jnp.int32, (8, LANES), 0)
    blank = jnp.zeros((8, LANES), jnp.float32)
    low, high = [blank] * DENSE, [blank] * DENSE
    for strip in range(STRIPS):
        for dense, place, slot, row, at in units(strip):
            to = PAIR * slot + EDGE * place
            turned = turn(span[row, at:at + 8], to)
            back = (to - EDGE) % LANES
            take_low, take_high = between(lane, to, to + EDGE), between(lane, back, back + EDGE)
            if dense == DENSE - 1:
                take_low, take_high = take_low & (sublane == strip), take_high & (sublane == strip)
            low[dense] = jnp.where(take_low, turned, low[dense])
            high[dense] = jnp.where(take_high, turned, high[dense])
        for dense in (2 * strip, 2 * strip + 1):
            low_edge[dense] = low[dense]
            high_edge[dense] = high[dense]
    low_edge[DENSE - 1] = low[-1]
    high_edge[DENSE - 1] = high[-1]


def own_kernel(span, basis, inv_root, scale, moments, strip_root, strip_source, strip_fixed, g, diag, *t):
    def start(i):
        row = i + 1
        root = span[row, :LAYERS]
        total = neighbours(root, span[row - 1, :LAYERS], span[row + 1, :LAYERS])
        fixed = span[row, 2 * LAYERS:2 * LAYERS + 1]
        d, g_row, t_row = start_fields(root, span[row, LAYERS:2 * LAYERS], fixed, total)
        return [(diag, i, d), (g, i, g_row), (t[0], i, t_row)]

    rows_in_blocks(FIRST, 3, start)

    for j, unroll in zip(range(1, ITERS + 1), (4, 7, 6, 5)):
        def step(i, j=j):
            new = g[i + j] * neighbours(t[j - 1][i + 1], t[j - 1][i], t[j - 1][i + 2])
            return [(t[j], i, new if j == 1 else 2.0 * new - t[j - 2][i + 2])]

        rows_in_blocks(FIRST - 2 * j, unroll, step)

    wide = lane_index(LAYERS)
    inner = between(wide, MERGE, LANES - MERGE)
    unroll = 2

    def finish(k, totals):
        stores = []
        for m in range(unroll):
            i = k * unroll + m
            fields = [t[j][i + LEAD - j] for j in range(ITERS + 1)]
            sums = neighbours(t[ITERS][i + 1], t[ITERS][i], t[ITERS][i + 2])
            fields.append(2.0 * g[i + LEAD] * sums - fields[ITERS - 1])
            inv, ratio = outer_factors(span[i + DEPTH, :LAYERS], diag[i + LEAD])
            stores += [(basis, (j, i), fields[j]) for j in range(BASIS)]
            stores += [(inv_root, i, inv), (scale, i, ratio)]
            new = products(jnp.where(inner, ratio * inv, 0.0), fields)
            totals = tuple(a + b for a, b in zip(totals, new))
        for ref, where, value in stores:
            ref[where] = value
        return totals

    zero = jnp.zeros((LAYERS, LANES), jnp.float32)
    moments[...] = as_row(lax.fori_loop(0, ROWS // unroll, finish, (zero,) * (2 * ITERS)))

    lane = lane_index(8)
    sublane = lax.broadcasted_iota(jnp.int32, (8, LANES), 0)
    heads = jnp.zeros((8, LANES), jnp.float32)
    for strip in range(STRIPS):
        for unit in range(2 * TILES + 1):
            tile = jnp.zeros((8, LANES), jnp.float32)
            for slot in range(FOLD):
                row = slot * STRIPS + strip
                if row < SPAN:
                    source, base = span[row, 8 * unit:8 * unit + 8], PAIR * slot
                    low, high = turn(source, base + EDGE), turn(source, base + PAIR - EDGE)
                    tile = jnp.where(between(lane, base + EDGE, base + SIDE), low, tile)
                    tile = jnp.where(between(lane, base + SIDE, base + PAIR - EDGE), high, tile)
            if unit < TILES:
                strip_root[strip, 8 * unit:8 * unit + 8] = tile
            elif unit < 2 * TILES:
                strip_source[strip, 8 * unit - LAYERS:8 * unit - LAYERS + 8] = tile
            else:
                heads = jnp.where(sublane == strip, tile, heads)
    strip_fixed[...] = heads


def strips_kernel(own_moments, own_root, own_source, own_fixed, from_low, from_high,
                  basis, inv_root, scale, moments, root, source, g):
    lane = lane_index(8)
    low_lanes = high_lanes = lane < 0
    for slot in range(FOLD):
        base = PAIR * slot
        low_lanes = low_lanes | between(lane, base, base + EDGE)
        high_lanes = high_lanes | between(lane, base + PAIR - EDGE, base + PAIR)

    def with_halo(own, dense, place=0):
        low = turn(from_low[dense], EDGE - EDGE * place)
        high = turn(from_high[dense], PAIR - EDGE - EDGE * place)
        return jnp.where(low_lanes, low, jnp.where(high_lanes, high, own))

    fixed = with_halo(own_fixed[...], DENSE - 1)
    for q in range(STRIPS):
        for k in range(TILES):
            tile = pl.ds(8 * k, 8)
            root[q, tile] = with_halo(own_root[q, tile], 2 * q, k)
            source[q, tile] = with_halo(own_source[q, tile], 2 * q + 1, k)

    def sums(ref, at):
        rows = [ref[(*at, q)] for q in range(STRIPS)]
        before = [turn(rows[-1], PAIR)] + rows[:-1]
        after = rows[1:] + [turn(rows[0], -PAIR)]
        return [neighbours(*three) for three in zip(rows, before, after)]

    wide = lane_index(LAYERS)
    own_lanes = []
    for slot in range(2):
        base = PAIR * slot
        low = between(wide, base + EDGE, base + EDGE + MERGE)
        own_lanes.append(low | between(wide, base + PAIR - EDGE - MERGE, base + PAIR - EDGE))

    weights = []
    for q, total in enumerate(sums(root, ())):
        d, g[q], basis[0, q] = start_fields(root[q], source[q], fixed[q:q + 1], total)
        inv, ratio = outer_factors(root[q], d)
        inv_root[q] = inv
        scale[q] = ratio
    for j in range(1, BASIS):
        for q, total in enumerate(sums(basis, (j - 1,))):
            new = g[q] * total
            basis[j, q] = new if j == 1 else 2.0 * new - basis[j - 2, q]

    totals = None
    for q in range(STRIPS):
        mine = own_lanes[1] | own_lanes[0] if q == DEPTH else own_lanes[1]
        new = products(jnp.where(mine, scale[q] * inv_root[q], 0.0), [basis[j, q] for j in range(ITERS + 1)])
        totals = new if totals is None else [a + b for a, b in zip(totals, new)]
    moments[...] = own_moments[...] + as_row(totals)


def added(a, b, factor):
    out = []
    for i in range(max(len(a), len(b))):
        left = a[i] if i < len(a) else None
        right = b[i] if i < len(b) else None
        if right is not None:
            right = factor * right
        out.append(right if left is None else left if right is None else left + right)
    return out


def shifted(a):
    out = [None] * (len(a) + 1)

    def put(i, value):
        out[i] = value if out[i] is None else out[i] + value

    for i, value in enumerate(a):
        if i == 0:
            put(1, value)
        else:
            put(i + 1, 0.5 * value)
            put(i - 1, 0.5 * value)
    return out


def form(a, b, gram):
    total = None
    for i, left in enumerate(a):
        inner = None
        for j, right in enumerate(b):
            if right is None:
                continue
            term = right * gram(i, j)
            inner = term if inner is None else inner + term
        inner = left * inner
        total = inner if total is None else total + inner
    return total


def recursion(moments):
    half = [0.5 * m for m in moments]

    def gram(i, j):
        return moments[i] if j == 0 else moments[j] if i == 0 else half[i + j] + half[abs(i - j)]

    one = jnp.ones_like(moments[0])
    precond, direction, head = [one], [], []
    gamma_old = alpha_old = None
    for step in range(ITERS):
        gamma = form(precond, precond, gram)
        delta = gamma - form(precond, shifted(precond), gram)
        if step == 0:
            direction = precond
            alpha = gamma / delta
        else:
            beta = gamma / gamma_old
            alpha = gamma / (delta - beta * gamma / alpha_old)
            direction = added(precond, direction, beta)
        head = added(head, direction, alpha)
        moved = added(direction, shifted(direction), -1.0)
        precond = added(precond, moved, -alpha)
        gamma_old, alpha_old = gamma, alpha
    return head, precond, added(precond, shifted(precond), -1.0)


def combine_kernel(moments, basis, inv_root, scale, strip_basis, strip_inv_root, strip_scale,
                   head_field, residual, applied, h_buf, r_buf, a_buf, sems):
    row = jnp.sum(moments[...], axis=0)
    column = lane_index(1)
    raw = []
    for n in range(2 * ITERS):
        value = jnp.sum(jnp.where(column == n, row, 0.0), axis=1, keepdims=True)
        raw.append(jnp.broadcast_to(value, (8, LANES)))
    full = raw[:2]
    for n in range(2, 2 * ITERS):
        full.append(2.0 * raw[n] - raw[n % 2])
    lane = lane_index(LAYERS)
    low, high = lane < MERGE, lane >= LANES - MERGE
    targets = (
        (h_buf, head_field, inv_root, strip_inv_root),
        (r_buf, residual, scale, strip_scale),
        (a_buf, applied, scale, strip_scale),
    )
    copies = []
    for n, (weights, (buf, out, factor, strip_factor)) in enumerate(zip(recursion(full), targets)):
        weights = [jnp.concatenate([w] * TILES, axis=0) for w in weights]

        def total(fields, factors, at):
            value = weights[0] * fields[0, at]
            for j in range(1, len(weights)):
                value = value + weights[j] * fields[j, at]
            return factors[at] * value

        strips = [total(strip_basis, strip_factor, q) for q in range(STRIPS)]
        for row in range(ROWS):
            slot, q = divmod(row + DEPTH, STRIPS)
            base = PAIR * slot
            value = total(basis, factor, row)
            value = jnp.where(low, turn(strips[q], -base - EDGE), value)
            value = jnp.where(high, turn(strips[q], LANES - (base + PAIR - EDGE)), value)
            for k in range(TILES):
                buf[pl.ds(k * ROWS + row, 8, stride=TILES * ROWS)] = value[8 * k:8 * k + 8]
        copies.append(pltpu.make_async_copy(buf, out, sems.at[n]))
        copies[-1].start()
    for copy in copies:
        copy.wait()


def f32(*shape):
    return jax.ShapeDtypeStruct(shape, jnp.float32)


def scratch(*shape):
    return pltpu.VMEM(shape, jnp.float32)


VMEM = pl.BlockSpec(memory_space=pltpu.VMEM)
HBM = pl.BlockSpec(memory_space=pltpu.HBM)


def call(kernel, outs, scratches=(), ins=VMEM, out=VMEM):
    def run(*args):
        return pl.pallas_call(
            kernel,
            out_shape=outs,
            in_specs=[ins] * len(args),
            out_specs=[out] * len(outs),
            scratch_shapes=list(scratches),
            compiler_params=pltpu.CompilerParams(vmem_limit_bytes=32 * 1024 * 1024),
        )(*args)

    return run


def prepare(recharge, conduct, top_layer, fixed_head):
    flat = (LAYERS * ROWS, LANES)
    plane = pltpu.VMEM((ROWS, LANES), jnp.int32)
    args = (recharge.reshape(flat), conduct.reshape(flat), top_layer, fixed_head)
    return call(
        prepare_kernel,
        (f32(ROWS, WIDTH, LANES), f32(FAR, LANES)),
        [scratch(*flat), scratch(*flat), plane, plane, pltpu.SemaphoreType.DMA((4,))],
        ins=HBM,
    )(*[pltpu.with_memory_space_constraint(a, pltpu.HBM) for a in args])


def edges(both, far):
    dense = f32(DENSE, 8, LANES)
    return call(edges_kernel, (f32(SPAN, WIDTH, LANES), dense, dense))(both, far)


def own_columns(span):
    field, strip = f32(ROWS, LAYERS, LANES), f32(STRIPS, LAYERS, LANES)
    outs = (f32(BASIS, ROWS, LAYERS, LANES), field, field, f32(1, LANES), strip, strip, f32(8, LANES))
    scratches = [scratch(FIRST, LAYERS, LANES)] * 2
    scratches += [scratch(FIRST - 2 * j, LAYERS, LANES) for j in range(ITERS + 1)]
    return call(own_kernel, outs, scratches)(span)


def strip_columns(moments, own, from_low, from_high):
    field = f32(STRIPS, LAYERS, LANES)
    outs = (f32(BASIS, STRIPS, LAYERS, LANES), field, field, f32(1, LANES))
    return call(strips_kernel, outs, [scratch(STRIPS, LAYERS, LANES)] * 3)(moments, *own, from_low, from_high)


def combine(moments, own, strips):
    flat = (LAYERS * ROWS, LANES)
    outs = call(
        combine_kernel,
        (f32(*flat),) * 3,
        [scratch(*flat)] * 3 + [pltpu.SemaphoreType.DMA((3,))],
        out=HBM,
    )(moments, *own, *strips)
    return tuple(out.reshape(LAYERS, ROWS, LANES) for out in outs)


def shift_both(low_going, high_going, axis):
    count = lax.axis_size(axis)
    up = [(i, i + 1) for i in range(count - 1)]
    down = [(target, source) for source, target in up]
    return lax.ppermute(high_going, axis, up), lax.ppermute(low_going, axis, down)


def between_chips(array):
    count = lax.axis_size(GX)
    pairs = []
    for i in range(1, count - 1, 2):
        pairs += [(i, i + 1), (i + 1, i)]
    return lax.ppermute(array, GX, pairs)


def spread_sum(row, axes, leader):
    count = lax.axis_size(axes)
    group = [(leader + i) % count for i in range(count)]
    rows = jnp.broadcast_to(row[None], (count,) + row.shape)
    return lax.all_to_all(rows, axes, 0, 0, axis_index_groups=[group], tiled=True)


def local(recharge, conduct, top_layer, fixed_head):
    main, part = prepare(recharge, conduct, top_layer, fixed_head)
    far = between_chips(part)
    both = lax.all_gather(main, "c", axis=0, tiled=True)
    span, low_edge, high_edge = edges(both, far)
    from_low, from_high = shift_both(low_edge, high_edge, "y")
    *own, own_moments, root, source, fixed = own_columns(span)
    *strips, moments = strip_columns(own_moments, (root, source, fixed), from_low, from_high)
    moments = jnp.sum(spread_sum(moments, ("z", "c"), 7 * 2 + 1), axis=0)
    moments = spread_sum(moments, ("x", "y"), 2 * 8 + 4)
    return combine(moments, own, strips)


def solution(mesh):
    grid = Mesh(mesh.devices.reshape(12, 4, 2, 8), ("z", "x", "c", "y"))
    field, plane = P(None, GX, "y"), P(GX, "y")
    return jax.shard_map(
        local, mesh=grid, in_specs=(field, field, plane, plane), out_specs=(field, field, field), check_vma=False
    )
```

```python
import jax
import jax.numpy as jnp
from jax import lax
from jax.experimental import pallas as pl
from jax.experimental.pallas import tpu as pltpu
from jax.sharding import Mesh, PartitionSpec as P

ITERS = 4
LAYERS = 48
ROWS = 8
LANES = 128
BASIS = ITERS + 2
DEPTH = BASIS
SPAN = ROWS + 2 * DEPTH
WIDTH = 2 * LAYERS + 8
TILES = LAYERS // 8
FIRST = SPAN - 2
LEAD = (FIRST - ROWS) // 2

EDGE = 7
SIDE = 3 * EDGE
PAIR = 2 * SIDE
FOLD = 3
STRIPS = 7
DENSE = 2 * STRIPS + 1
FAR = (2 * DEPTH - 1) * LAYERS + 8
MERGE = 8

store_term = 0.1
boundary_term = 4.0
vertical_ratio = 0.3

GX = ("z", "x", "c")


def lane_index(rows):
    return lax.broadcasted_iota(jnp.int32, (rows, LANES), 1)


def turn(tile, lanes):
    lanes %= LANES
    return pltpu.roll(tile, lanes, 1) if lanes else tile


def between(lane, low, high):
    return (lane >= low) & (lane < high)


def layer_above(row):
    sublane = lax.broadcasted_iota(jnp.int32, (8, LANES), 0)
    edge = jnp.where(sublane == 0, 0.0, pltpu.roll(row[LAYERS - 8:], 1, 0))
    return jnp.concatenate([edge, row[:LAYERS - 8]], axis=0)


def layer_below(row):
    sublane = lax.broadcasted_iota(jnp.int32, (8, LANES), 0)
    edge = jnp.where(sublane == 7, 0.0, pltpu.roll(row[:8], 7, 0))
    return jnp.concatenate([row[8:], edge], axis=0)


def neighbours(row, before, after):
    sides = turn(row, 1) + turn(row, -1) + before + after
    return sides + vertical_ratio * (layer_above(row) + layer_below(row))


def start_fields(root, source, fixed, total):
    head = jnp.where(layer_above(root) > 0.0, 0.0, boundary_term * fixed)
    diagonal = jnp.where(root > 0.0, root * total + (store_term + head), 1.0)
    inverse = 1.0 / diagonal
    return diagonal, root * root * inverse, source * inverse


def outer_factors(root, diagonal):
    inv = jnp.where(root > 0.0, 1.0 / root, 0.0)
    return inv, diagonal * inv


def products(weight, fields):
    out = []
    for j in range(ITERS):
        weighted = weight * fields[j]
        out += [weighted * fields[j], weighted * fields[j + 1]]
    return out


def as_row(totals):
    column = lane_index(1)
    row = jnp.zeros((1, LANES), jnp.float32)
    for n, total in enumerate(totals):
        row = jnp.where(column == n, jnp.sum(jnp.sum(total, axis=0, keepdims=True), axis=1, keepdims=True), row)
    return row


def rows_in_blocks(count, unroll, step):
    def block(k, _):
        stores = []
        for m in range(unroll):
            stores += step(k * unroll + m)
        for ref, where, value in stores:
            ref[where] = value
        return 0

    lax.fori_loop(0, count // unroll, block, 0)


def prepare_kernel(recharge, conduct, top_layer, fixed_head, main, part, r_buf, c_buf, t_buf, f_buf, sems):
    pairs = ((conduct, c_buf), (top_layer, t_buf), (recharge, r_buf), (fixed_head, f_buf))
    copies = [pltpu.make_async_copy(a, b, sems.at[n]) for n, (a, b) in enumerate(pairs)]
    for copy in copies:
        copy.start()
    core = lax.axis_index("c")
    level = TILES * lax.broadcasted_iota(jnp.int32, (8, LANES), 0)
    tiles = [(row, k, pl.ds(k * ROWS + row, 8, stride=TILES * ROWS)) for row in range(ROWS) for k in range(TILES)]
    copies[0].wait()
    copies[1].wait()
    for row, k, layers in tiles:
        root = jnp.where(level + k >= t_buf[row:row + 1], jnp.sqrt(c_buf[layers]), 0.0)
        main[row, 8 * k:8 * k + 8] = root
    nearest = [jnp.where(core == 0, n, ROWS - 1 - n) for n in range(DEPTH)]
    for n, row in enumerate(nearest):
        part[n * LAYERS:(n + 1) * LAYERS] = main[row, :LAYERS]
    copies[2].wait()
    copies[3].wait()
    for row, k, layers in tiles:
        main[row, LAYERS + 8 * k:LAYERS + 8 * k + 8] = main[row, 8 * k:8 * k + 8] * r_buf[layers]
    for n, row in enumerate(nearest[:-1]):
        part[(DEPTH + n) * LAYERS:(DEPTH + n + 1) * LAYERS] = main[row, LAYERS:2 * LAYERS]
    fixed = f_buf[...].astype(jnp.float32)
    part[FAR - 8:] = fixed
    for row in range(ROWS):
        main[row, 2 * LAYERS:] = jnp.broadcast_to(fixed[row:row + 1], (8, LANES))


def units(strip):
    for slot in range(FOLD):
        row = slot * STRIPS + strip
        if row < SPAN:
            for unit in range(2 * TILES):
                group, place = divmod(unit, TILES)
                yield 2 * strip + group, place, slot, row, 8 * unit
            yield DENSE - 1, 0, slot, row, 2 * LAYERS


def edges_kernel(both, far, span, first_edge, second_edge):
    even = lax.rem(lax.axis_index("y"), 2) == 0

    def put(dense, low, high):
        first_edge[dense] = jnp.where(even, high, low)
        second_edge[dense] = jnp.where(even, low, high)

    core = lax.axis_index("c")
    for n in range(ROWS + DEPTH):
        span[DEPTH * (1 - core) + n] = both[(ROWS - DEPTH) * core + n]
    for n in range(DEPTH):
        row = jnp.where(core == 0, DEPTH - 1 - n, ROWS + DEPTH + n)
        span[row, :LAYERS] = far[n * LAYERS:(n + 1) * LAYERS]
        if n < DEPTH - 1:
            span[row, LAYERS:2 * LAYERS] = far[(DEPTH + n) * LAYERS:(DEPTH + n + 1) * LAYERS]
        else:
            span[row, LAYERS:2 * LAYERS] = jnp.zeros((LAYERS, LANES), jnp.float32)
        fixed = far[pl.ds(FAR - 8 + jnp.where(core == 0, ROWS - 1 - n, n), 1)]
        span[row, 2 * LAYERS:] = jnp.broadcast_to(fixed, (8, LANES))
    lane = lane_index(8)
    sublane = lax.broadcasted_iota(jnp.int32, (8, LANES), 0)
    blank = jnp.zeros((8, LANES), jnp.float32)
    low, high = [blank] * DENSE, [blank] * DENSE
    for strip in range(STRIPS):
        for dense, place, slot, row, at in units(strip):
            to = PAIR * slot + EDGE * place
            turned = turn(span[row, at:at + 8], to)
            back = (to - EDGE) % LANES
            take_low, take_high = between(lane, to, to + EDGE), between(lane, back, back + EDGE)
            if dense == DENSE - 1:
                take_low, take_high = take_low & (sublane == strip), take_high & (sublane == strip)
            low[dense] = jnp.where(take_low, turned, low[dense])
            high[dense] = jnp.where(take_high, turned, high[dense])
        for dense in (2 * strip, 2 * strip + 1):
            put(dense, low[dense], high[dense])
    put(DENSE - 1, low[-1], high[-1])


def own_kernel(span, basis, inv_root, scale, moments, strip_root, strip_source, strip_fixed, g, diag, *t):
    def start(i):
        row = i + 1
        root = span[row, :LAYERS]
        total = neighbours(root, span[row - 1, :LAYERS], span[row + 1, :LAYERS])
        fixed = span[row, 2 * LAYERS:2 * LAYERS + 1]
        d, g_row, t_row = start_fields(root, span[row, LAYERS:2 * LAYERS], fixed, total)
        return [(diag, i, d), (g, i, g_row), (t[0], i, t_row)]

    rows_in_blocks(FIRST, 3, start)

    for j, unroll in zip(range(1, ITERS + 1), (4, 7, 6, 5)):
        def step(i, j=j):
            new = g[i + j] * neighbours(t[j - 1][i + 1], t[j - 1][i], t[j - 1][i + 2])
            return [(t[j], i, new if j == 1 else 2.0 * new - t[j - 2][i + 2])]

        rows_in_blocks(FIRST - 2 * j, unroll, step)

    wide = lane_index(LAYERS)
    inner = between(wide, MERGE, LANES - MERGE)
    unroll = 2

    def finish(k, totals):
        stores = []
        for m in range(unroll):
            i = k * unroll + m
            fields = [t[j][i + LEAD - j] for j in range(ITERS + 1)]
            sums = neighbours(t[ITERS][i + 1], t[ITERS][i], t[ITERS][i + 2])
            fields.append(2.0 * g[i + LEAD] * sums - fields[ITERS - 1])
            inv, ratio = outer_factors(span[i + DEPTH, :LAYERS], diag[i + LEAD])
            stores += [(basis, (j, i), fields[j]) for j in range(BASIS)]
            stores += [(inv_root, i, inv), (scale, i, ratio)]
            new = products(jnp.where(inner, ratio * inv, 0.0), fields)
            totals = tuple(a + b for a, b in zip(totals, new))
        for ref, where, value in stores:
            ref[where] = value
        return totals

    zero = jnp.zeros((LAYERS, LANES), jnp.float32)
    moments[...] = as_row(lax.fori_loop(0, ROWS // unroll, finish, (zero,) * (2 * ITERS)))

    lane = lane_index(8)
    sublane = lax.broadcasted_iota(jnp.int32, (8, LANES), 0)
    heads = jnp.zeros((8, LANES), jnp.float32)
    for strip in range(STRIPS):
        for unit in range(2 * TILES + 1):
            tile = jnp.zeros((8, LANES), jnp.float32)
            for slot in range(FOLD):
                row = slot * STRIPS + strip
                if row < SPAN:
                    source, base = span[row, 8 * unit:8 * unit + 8], PAIR * slot
                    low, high = turn(source, base + EDGE), turn(source, base + PAIR - EDGE)
                    tile = jnp.where(between(lane, base + EDGE, base + SIDE), low, tile)
                    tile = jnp.where(between(lane, base + SIDE, base + PAIR - EDGE), high, tile)
            if unit < TILES:
                strip_root[strip, 8 * unit:8 * unit + 8] = tile
            elif unit < 2 * TILES:
                strip_source[strip, 8 * unit - LAYERS:8 * unit - LAYERS + 8] = tile
            else:
                heads = jnp.where(sublane == strip, tile, heads)
    strip_fixed[...] = heads


def strips_kernel(own_moments, own_root, own_source, own_fixed, first_edge, second_edge,
                  basis, inv_root, scale, moments, root, source, g):
    lane = lane_index(8)
    low_lanes = high_lanes = lane < 0
    for slot in range(FOLD):
        base = PAIR * slot
        low_lanes = low_lanes | between(lane, base, base + EDGE)
        high_lanes = high_lanes | between(lane, base + PAIR - EDGE, base + PAIR)

    even = lax.rem(lax.axis_index("y"), 2) == 0

    def from_sides(dense):
        first, second = first_edge[dense], second_edge[dense]
        return jnp.where(even, second, first), jnp.where(even, first, second)

    def with_halo(own, sides, place=0):
        low = turn(sides[0], EDGE - EDGE * place)
        high = turn(sides[1], PAIR - EDGE - EDGE * place)
        return jnp.where(low_lanes, low, jnp.where(high_lanes, high, own))

    fixed = with_halo(own_fixed[...], from_sides(DENSE - 1))
    for q in range(STRIPS):
        root_sides, source_sides = from_sides(2 * q), from_sides(2 * q + 1)
        for k in range(TILES):
            tile = pl.ds(8 * k, 8)
            root[q, tile] = with_halo(own_root[q, tile], root_sides, k)
            source[q, tile] = with_halo(own_source[q, tile], source_sides, k)

    def sums(ref, at):
        rows = [ref[(*at, q)] for q in range(STRIPS)]
        before = [turn(rows[-1], PAIR)] + rows[:-1]
        after = rows[1:] + [turn(rows[0], -PAIR)]
        return [neighbours(*three) for three in zip(rows, before, after)]

    wide = lane_index(LAYERS)
    own_lanes = []
    for slot in range(2):
        base = PAIR * slot
        low = between(wide, base + EDGE, base + EDGE + MERGE)
        own_lanes.append(low | between(wide, base + PAIR - EDGE - MERGE, base + PAIR - EDGE))

    weights = []
    for q, total in enumerate(sums(root, ())):
        d, g[q], basis[0, q] = start_fields(root[q], source[q], fixed[q:q + 1], total)
        inv, ratio = outer_factors(root[q], d)
        inv_root[q] = inv
        scale[q] = ratio
    for j in range(1, BASIS):
        for q, total in enumerate(sums(basis, (j - 1,))):
            new = g[q] * total
            basis[j, q] = new if j == 1 else 2.0 * new - basis[j - 2, q]

    totals = None
    for q in range(STRIPS):
        mine = own_lanes[1] | own_lanes[0] if q == DEPTH else own_lanes[1]
        new = products(jnp.where(mine, scale[q] * inv_root[q], 0.0), [basis[j, q] for j in range(ITERS + 1)])
        totals = new if totals is None else [a + b for a, b in zip(totals, new)]
    moments[...] = own_moments[...] + as_row(totals)


def added(a, b, factor):
    out = []
    for i in range(max(len(a), len(b))):
        left = a[i] if i < len(a) else None
        right = b[i] if i < len(b) else None
        if right is not None:
            right = factor * right
        out.append(right if left is None else left if right is None else left + right)
    return out


def shifted(a):
    out = [None] * (len(a) + 1)

    def put(i, value):
        out[i] = value if out[i] is None else out[i] + value

    for i, value in enumerate(a):
        if i == 0:
            put(1, value)
        else:
            put(i + 1, 0.5 * value)
            put(i - 1, 0.5 * value)
    return out


def form(a, b, gram):
    total = None
    for i, left in enumerate(a):
        inner = None
        for j, right in enumerate(b):
            if right is None:
                continue
            term = right * gram(i, j)
            inner = term if inner is None else inner + term
        inner = left * inner
        total = inner if total is None else total + inner
    return total


def recursion(moments):
    half = [0.5 * m for m in moments]

    def gram(i, j):
        return moments[i] if j == 0 else moments[j] if i == 0 else half[i + j] + half[abs(i - j)]

    one = jnp.ones_like(moments[0])
    precond, direction, head = [one], [], []
    gamma_old = alpha_old = None
    for step in range(ITERS):
        gamma = form(precond, precond, gram)
        delta = gamma - form(precond, shifted(precond), gram)
        if step == 0:
            direction = precond
            alpha = gamma / delta
        else:
            beta = gamma / gamma_old
            alpha = gamma / (delta - beta * gamma / alpha_old)
            direction = added(precond, direction, beta)
        head = added(head, direction, alpha)
        moved = added(direction, shifted(direction), -1.0)
        precond = added(precond, moved, -alpha)
        gamma_old, alpha_old = gamma, alpha
    return head, precond, added(precond, shifted(precond), -1.0)


def combine_kernel(moments, basis, inv_root, scale, strip_basis, strip_inv_root, strip_scale,
                   head_field, residual, applied, h_buf, r_buf, a_buf, sems):
    row = jnp.sum(moments[...], axis=0)
    column = lane_index(1)
    raw = []
    for n in range(2 * ITERS):
        value = jnp.sum(jnp.where(column == n, row, 0.0), axis=1, keepdims=True)
        raw.append(jnp.broadcast_to(value, (8, LANES)))
    full = raw[:2]
    for n in range(2, 2 * ITERS):
        full.append(2.0 * raw[n] - raw[n % 2])
    lane = lane_index(LAYERS)
    low, high = lane < MERGE, lane >= LANES - MERGE
    targets = (
        (h_buf, head_field, inv_root, strip_inv_root),
        (r_buf, residual, scale, strip_scale),
        (a_buf, applied, scale, strip_scale),
    )
    copies = []
    for n, (weights, (buf, out, factor, strip_factor)) in enumerate(zip(recursion(full), targets)):
        weights = [jnp.concatenate([w] * TILES, axis=0) for w in weights]

        def total(fields, factors, at):
            value = weights[0] * fields[0, at]
            for j in range(1, len(weights)):
                value = value + weights[j] * fields[j, at]
            return factors[at] * value

        strips = [total(strip_basis, strip_factor, q) for q in range(STRIPS)]
        for row in range(ROWS):
            slot, q = divmod(row + DEPTH, STRIPS)
            base = PAIR * slot
            value = total(basis, factor, row)
            value = jnp.where(low, turn(strips[q], -base - EDGE), value)
            value = jnp.where(high, turn(strips[q], LANES - (base + PAIR - EDGE)), value)
            for k in range(TILES):
                buf[pl.ds(k * ROWS + row, 8, stride=TILES * ROWS)] = value[8 * k:8 * k + 8]
        copies.append(pltpu.make_async_copy(buf, out, sems.at[n]))
        copies[-1].start()
    for copy in copies:
        copy.wait()


def f32(*shape):
    return jax.ShapeDtypeStruct(shape, jnp.float32)


def scratch(*shape):
    return pltpu.VMEM(shape, jnp.float32)


VMEM = pl.BlockSpec(memory_space=pltpu.VMEM)
HBM = pl.BlockSpec(memory_space=pltpu.HBM)


def call(kernel, outs, scratches=(), ins=VMEM, out=VMEM):
    def run(*args):
        return pl.pallas_call(
            kernel,
            out_shape=outs,
            in_specs=[ins] * len(args),
            out_specs=[out] * len(outs),
            scratch_shapes=list(scratches),
            compiler_params=pltpu.CompilerParams(vmem_limit_bytes=32 * 1024 * 1024),
        )(*args)

    return run


def prepare(recharge, conduct, top_layer, fixed_head):
    flat = (LAYERS * ROWS, LANES)
    plane = pltpu.VMEM((ROWS, LANES), jnp.int32)
    args = (recharge.reshape(flat), conduct.reshape(flat), top_layer, fixed_head)
    return call(
        prepare_kernel,
        (f32(ROWS, WIDTH, LANES), f32(FAR, LANES)),
        [scratch(*flat), scratch(*flat), plane, plane, pltpu.SemaphoreType.DMA((4,))],
        ins=HBM,
    )(*[pltpu.with_memory_space_constraint(a, pltpu.HBM) for a in args])


def edges(both, far):
    dense = f32(DENSE, 8, LANES)
    return call(edges_kernel, (f32(SPAN, WIDTH, LANES), dense, dense))(both, far)


def own_columns(span):
    field, strip = f32(ROWS, LAYERS, LANES), f32(STRIPS, LAYERS, LANES)
    outs = (f32(BASIS, ROWS, LAYERS, LANES), field, field, f32(1, LANES), strip, strip, f32(8, LANES))
    scratches = [scratch(FIRST, LAYERS, LANES)] * 2
    scratches += [scratch(FIRST - 2 * j, LAYERS, LANES) for j in range(ITERS + 1)]
    return call(own_kernel, outs, scratches)(span)


def strip_columns(moments, own, first_edge, second_edge):
    field = f32(STRIPS, LAYERS, LANES)
    outs = (f32(BASIS, STRIPS, LAYERS, LANES), field, field, f32(1, LANES))
    return call(strips_kernel, outs, [scratch(STRIPS, LAYERS, LANES)] * 3)(moments, *own, first_edge, second_edge)


def combine(moments, own, strips):
    flat = (LAYERS * ROWS, LANES)
    outs = call(
        combine_kernel,
        (f32(*flat),) * 3,
        [scratch(*flat)] * 3 + [pltpu.SemaphoreType.DMA((3,))],
        out=HBM,
    )(moments, *own, *strips)
    return tuple(out.reshape(LAYERS, ROWS, LANES) for out in outs)


def swap(array, axis, start):
    pairs = []
    for i in range(start, lax.axis_size(axis) - 1, 2):
        pairs += [(i, i + 1), (i + 1, i)]
    return lax.ppermute(array, axis, pairs)


def spread_sum(row, axes, leader):
    count = lax.axis_size(axes)
    group = [(leader + i) % count for i in range(count)]
    rows = jnp.broadcast_to(row[None], (count,) + row.shape)
    return lax.all_to_all(rows, axes, 0, 0, axis_index_groups=[group], tiled=True)


def local(recharge, conduct, top_layer, fixed_head):
    main, part = prepare(recharge, conduct, top_layer, fixed_head)
    far = swap(part, GX, 1)
    both = lax.all_gather(main, "c", axis=0, tiled=True)
    span, first_edge, second_edge = edges(both, far)
    first_edge = swap(first_edge, "y", 0)
    second_edge = swap(second_edge, "y", 1)
    *own, own_moments, root, source, fixed = own_columns(span)
    *strips, moments = strip_columns(own_moments, (root, source, fixed), first_edge, second_edge)
    moments = jnp.sum(spread_sum(moments, ("z", "c"), 7 * 2 + 1), axis=0)
    moments = spread_sum(moments, ("x", "y"), 2 * 8 + 4)
    return combine(moments, own, strips)


def solution(mesh):
    grid = Mesh(mesh.devices.reshape(12, 4, 2, 8), ("z", "x", "c", "y"))
    field, plane = P(None, GX, "y"), P(GX, "y")
    return jax.shard_map(
        local, mesh=grid, in_specs=(field, field, plane, plane), out_specs=(field, field, field), check_vma=False
    )
```

```python
import jax
import jax.numpy as jnp
from jax import lax
from jax.experimental import pallas as pl
from jax.experimental.pallas import tpu as pltpu
from jax.sharding import Mesh, PartitionSpec as P

ITERS = 4
LAYERS = 48
ROWS = 8
LANES = 128
BASIS = ITERS + 2
DEPTH = BASIS
SPAN = ROWS + 2 * DEPTH
WIDTH = 2 * LAYERS + 8
TILES = LAYERS // 8
FIRST = SPAN - 2
LEAD = (FIRST - ROWS) // 2

EDGE = 7
SIDE = 3 * EDGE
PAIR = 2 * SIDE
FOLD = 3
STRIPS = 7
DENSE = 2 * STRIPS + 1
FAR = (2 * DEPTH - 1) * LAYERS + 8
MERGE = 8

store_term = 0.1
boundary_term = 4.0
vertical_ratio = 0.3

GX = ("z", "x", "c")


def lane_index(rows):
    return lax.broadcasted_iota(jnp.int32, (rows, LANES), 1)


def turn(tile, lanes):
    lanes %= LANES
    return pltpu.roll(tile, lanes, 1) if lanes else tile


def between(lane, low, high):
    return (lane >= low) & (lane < high)


def layer_above(row):
    sublane = lax.broadcasted_iota(jnp.int32, (8, LANES), 0)
    edge = jnp.where(sublane == 0, 0.0, pltpu.roll(row[LAYERS - 8:], 1, 0))
    return jnp.concatenate([edge, row[:LAYERS - 8]], axis=0)


def layer_below(row):
    sublane = lax.broadcasted_iota(jnp.int32, (8, LANES), 0)
    edge = jnp.where(sublane == 7, 0.0, pltpu.roll(row[:8], 7, 0))
    return jnp.concatenate([row[8:], edge], axis=0)


def neighbours(row, before, after):
    sides = turn(row, 1) + turn(row, -1) + before + after
    return sides + vertical_ratio * (layer_above(row) + layer_below(row))


def start_fields(root, source, fixed, total):
    head = jnp.where(layer_above(root) > 0.0, 0.0, boundary_term * fixed)
    diagonal = jnp.where(root > 0.0, root * total + (store_term + head), 1.0)
    inverse = 1.0 / diagonal
    return diagonal, root * root * inverse, source * inverse


def outer_factors(root, diagonal):
    inv = jnp.where(root > 0.0, 1.0 / root, 0.0)
    return inv, diagonal * inv


def products(weight, fields):
    out = []
    for j in range(ITERS):
        weighted = weight * fields[j]
        out += [weighted * fields[j], weighted * fields[j + 1]]
    return out


def as_row(totals):
    column = lane_index(1)
    row = jnp.zeros((1, LANES), jnp.float32)
    for n, total in enumerate(totals):
        row = jnp.where(column == n, jnp.sum(jnp.sum(total, axis=0, keepdims=True), axis=1, keepdims=True), row)
    return row


def rows_in_blocks(count, unroll, step):
    def block(k, _):
        stores = []
        for m in range(unroll):
            stores += step(k * unroll + m)
        for ref, where, value in stores:
            ref[where] = value
        return 0

    lax.fori_loop(0, count // unroll, block, 0)


def prepare_kernel(recharge, conduct, top_layer, fixed_head, main, part, r_buf, c_buf, t_buf, f_buf, sems):
    pairs = ((conduct, c_buf), (top_layer, t_buf), (recharge, r_buf), (fixed_head, f_buf))
    copies = [pltpu.make_async_copy(a, b, sems.at[n]) for n, (a, b) in enumerate(pairs)]
    for copy in copies:
        copy.start()
    core = lax.axis_index("c")
    level = TILES * lax.broadcasted_iota(jnp.int32, (8, LANES), 0)
    tiles = [(row, k, pl.ds(k * ROWS + row, 8, stride=TILES * ROWS)) for row in range(ROWS) for k in range(TILES)]
    copies[0].wait()
    copies[1].wait()
    for row, k, layers in tiles:
        root = jnp.where(level + k >= t_buf[row:row + 1], jnp.sqrt(c_buf[layers]), 0.0)
        main[row, 8 * k:8 * k + 8] = root
    nearest = [jnp.where(core == 0, n, ROWS - 1 - n) for n in range(DEPTH)]
    for n, row in enumerate(nearest):
        part[n * LAYERS:(n + 1) * LAYERS] = main[row, :LAYERS]
    copies[2].wait()
    copies[3].wait()
    for row, k, layers in tiles:
        main[row, LAYERS + 8 * k:LAYERS + 8 * k + 8] = main[row, 8 * k:8 * k + 8] * r_buf[layers]
    for n, row in enumerate(nearest[:-1]):
        part[(DEPTH + n) * LAYERS:(DEPTH + n + 1) * LAYERS] = main[row, LAYERS:2 * LAYERS]
    fixed = f_buf[...].astype(jnp.float32)
    part[FAR - 8:] = fixed
    for row in range(ROWS):
        main[row, 2 * LAYERS:] = jnp.broadcast_to(fixed[row:row + 1], (8, LANES))


def on_each_core(body):
    core = lax.axis_index("c")
    for which in range(2):
        @pl.when(core == which)
        def _(which=which):
            near = range(DEPTH, SPAN) if which == 0 else range(SPAN - DEPTH)
            body(which, near, [row for row in range(SPAN) if row not in near])


def add_units(low, high, row, read):
    lane = lane_index(8)
    sublane = lax.broadcasted_iota(jnp.int32, (8, LANES), 0)
    slot, strip = divmod(row, STRIPS)
    for unit in range(2 * TILES + 1):
        group, place = divmod(unit, TILES)
        dense, to = 2 * strip + group, PAIR * slot + EDGE * place
        if unit == 2 * TILES:
            dense, to = DENSE - 1, PAIR * slot
        back = (to - EDGE) % LANES
        take_low, take_high = between(lane, to, to + EDGE), between(lane, back, back + EDGE)
        if dense == DENSE - 1:
            take_low, take_high = take_low & (sublane == strip), take_high & (sublane == strip)
        turned = turn(read(8 * unit), to)
        for tiles, take in ((low, take_low), (high, take_high)):
            tiles[dense] = jnp.where(take, turned, 0.0 if tiles[dense] is None else tiles[dense])


def add_own(tiles, row, read):
    lane = lane_index(8)
    sublane = lax.broadcasted_iota(jnp.int32, (8, LANES), 0)
    slot, strip = divmod(row, STRIPS)
    base = PAIR * slot
    for unit in range(2 * TILES + 1):
        source = read(8 * unit)
        key = (strip, unit) if unit < 2 * TILES else None
        take_low = between(lane, base + EDGE, base + SIDE)
        take_high = between(lane, base + SIDE, base + PAIR - EDGE)
        if key is None:
            take_low, take_high = take_low & (sublane == strip), take_high & (sublane == strip)
        tile = jnp.where(take_low, turn(source, base + EDGE), tiles.get(key, 0.0))
        tiles[key] = jnp.where(take_high, turn(source, base + PAIR - EDGE), tile)


def strip_place(refs, key):
    root, source, fixed = refs
    if key is None:
        return fixed, ...
    strip, unit = key
    ref = root if unit < TILES else source
    return ref, (strip, pl.ds(8 * (unit % TILES), 8))


def near_kernel(both, low_edge, high_edge, *strip_refs):
    def body(which, near, _):
        shift = -DEPTH if which == 0 else ROWS - DEPTH
        low, high, strips = [None] * DENSE, [None] * DENSE, {}
        for row in near:
            def read(at, row=row):
                return both[row + shift, at:at + 8]

            add_units(low, high, row, read)
            add_own(strips, row, read)
        for n in range(DENSE):
            low_edge[n] = low[n]
            high_edge[n] = high[n]
        for key, tile in strips.items():
            ref, at = strip_place(strip_refs, key)
            ref[at] = tile

    on_each_core(body)


def far_row(far, which, row):
    n = DEPTH - 1 - row if which == 0 else row - ROWS - DEPTH
    at = FAR - 8 + (ROWS - 1 - n if which == 0 else n)
    root = far[n * LAYERS:(n + 1) * LAYERS]
    if n < DEPTH - 1:
        source = far[(DEPTH + n) * LAYERS:(DEPTH + n + 1) * LAYERS]
    else:
        source = jnp.zeros((LAYERS, LANES), jnp.float32)
    return jnp.concatenate([root, source, jnp.broadcast_to(far[at:at + 1], (8, LANES))], axis=0)


def edges_kernel(near_low, near_high, far, first_edge, second_edge):
    even = lax.rem(lax.axis_index("y"), 2) == 0

    def body(which, _, rows):
        low, high = [near_low[n] for n in range(DENSE)], [near_high[n] for n in range(DENSE)]
        for row in rows:
            values = far_row(far, which, row)
            add_units(low, high, row, lambda at, values=values: values[at:at + 8])
        for n in range(DENSE):
            first_edge[n] = jnp.where(even, high[n], low[n])
            second_edge[n] = jnp.where(even, low[n], high[n])

    on_each_core(body)


def own_kernel(both, far, near_root, near_source, near_fixed, basis, inv_root, scale, moments,
               strip_root, strip_source, strip_fixed, span, g, diag, *t):
    def fill(which, near, rows):
        for row in near:
            span[row] = both[row - DEPTH if which == 0 else row + ROWS - DEPTH]
        for row in rows:
            span[row] = far_row(far, which, row)

    on_each_core(fill)

    def start(i):
        row = i + 1
        root = span[row, :LAYERS]
        total = neighbours(root, span[row - 1, :LAYERS], span[row + 1, :LAYERS])
        fixed = span[row, 2 * LAYERS:2 * LAYERS + 1]
        d, g_row, t_row = start_fields(root, span[row, LAYERS:2 * LAYERS], fixed, total)
        return [(diag, i, d), (g, i, g_row), (t[0], i, t_row)]

    rows_in_blocks(FIRST, 3, start)

    for j, unroll in zip(range(1, ITERS + 1), (4, 7, 6, 5)):
        def step(i, j=j):
            new = g[i + j] * neighbours(t[j - 1][i + 1], t[j - 1][i], t[j - 1][i + 2])
            return [(t[j], i, new if j == 1 else 2.0 * new - t[j - 2][i + 2])]

        rows_in_blocks(FIRST - 2 * j, unroll, step)

    wide = lane_index(LAYERS)
    inner = between(wide, MERGE, LANES - MERGE)
    unroll = 2

    def finish(k, totals):
        stores = []
        for m in range(unroll):
            i = k * unroll + m
            fields = [t[j][i + LEAD - j] for j in range(ITERS + 1)]
            sums = neighbours(t[ITERS][i + 1], t[ITERS][i], t[ITERS][i + 2])
            fields.append(2.0 * g[i + LEAD] * sums - fields[ITERS - 1])
            inv, ratio = outer_factors(span[i + DEPTH, :LAYERS], diag[i + LEAD])
            stores += [(basis, (j, i), fields[j]) for j in range(BASIS)]
            stores += [(inv_root, i, inv), (scale, i, ratio)]
            new = products(jnp.where(inner, ratio * inv, 0.0), fields)
            totals = tuple(a + b for a, b in zip(totals, new))
        for ref, where, value in stores:
            ref[where] = value
        return totals

    zero = jnp.zeros((LAYERS, LANES), jnp.float32)
    moments[...] = as_row(lax.fori_loop(0, ROWS // unroll, finish, (zero,) * (2 * ITERS)))

    strip_root[...] = near_root[...]
    strip_source[...] = near_source[...]
    strip_fixed[...] = near_fixed[...]
    refs = (strip_root, strip_source, strip_fixed)

    def body(which, _, rows):
        keys = [(row % STRIPS, unit) for row in rows for unit in range(2 * TILES)] + [None]
        tiles = {}
        for key in keys:
            ref, at = strip_place(refs, key)
            tiles[key] = ref[at]
        for row in rows:
            add_own(tiles, row, lambda at, row=row: span[row, at:at + 8])
        for key, tile in tiles.items():
            ref, at = strip_place(refs, key)
            ref[at] = tile

    on_each_core(body)


def strips_kernel(own_moments, own_root, own_source, own_fixed, first_edge, second_edge,
                  basis, inv_root, scale, moments, root, source, g):
    lane = lane_index(8)
    low_lanes = high_lanes = lane < 0
    for slot in range(FOLD):
        base = PAIR * slot
        low_lanes = low_lanes | between(lane, base, base + EDGE)
        high_lanes = high_lanes | between(lane, base + PAIR - EDGE, base + PAIR)

    even = lax.rem(lax.axis_index("y"), 2) == 0

    def from_sides(dense):
        first, second = first_edge[dense], second_edge[dense]
        return jnp.where(even, second, first), jnp.where(even, first, second)

    def with_halo(own, sides, place=0):
        low = turn(sides[0], EDGE - EDGE * place)
        high = turn(sides[1], PAIR - EDGE - EDGE * place)
        return jnp.where(low_lanes, low, jnp.where(high_lanes, high, own))

    fixed = with_halo(own_fixed[...], from_sides(DENSE - 1))
    for q in range(STRIPS):
        root_sides, source_sides = from_sides(2 * q), from_sides(2 * q + 1)
        for k in range(TILES):
            tile = pl.ds(8 * k, 8)
            root[q, tile] = with_halo(own_root[q, tile], root_sides, k)
            source[q, tile] = with_halo(own_source[q, tile], source_sides, k)

    def sums(ref, at):
        rows = [ref[(*at, q)] for q in range(STRIPS)]
        before = [turn(rows[-1], PAIR)] + rows[:-1]
        after = rows[1:] + [turn(rows[0], -PAIR)]
        return [neighbours(*three) for three in zip(rows, before, after)]

    wide = lane_index(LAYERS)
    own_lanes = []
    for slot in range(2):
        base = PAIR * slot
        low = between(wide, base + EDGE, base + EDGE + MERGE)
        own_lanes.append(low | between(wide, base + PAIR - EDGE - MERGE, base + PAIR - EDGE))

    weights = []
    for q, total in enumerate(sums(root, ())):
        d, g[q], basis[0, q] = start_fields(root[q], source[q], fixed[q:q + 1], total)
        inv, ratio = outer_factors(root[q], d)
        inv_root[q] = inv
        scale[q] = ratio
    for j in range(1, BASIS):
        for q, total in enumerate(sums(basis, (j - 1,))):
            new = g[q] * total
            basis[j, q] = new if j == 1 else 2.0 * new - basis[j - 2, q]

    totals = None
    for q in range(STRIPS):
        mine = own_lanes[1] | own_lanes[0] if q == DEPTH else own_lanes[1]
        new = products(jnp.where(mine, scale[q] * inv_root[q], 0.0), [basis[j, q] for j in range(ITERS + 1)])
        totals = new if totals is None else [a + b for a, b in zip(totals, new)]
    moments[...] = own_moments[...] + as_row(totals)


def added(a, b, factor):
    out = []
    for i in range(max(len(a), len(b))):
        left = a[i] if i < len(a) else None
        right = b[i] if i < len(b) else None
        if right is not None:
            right = factor * right
        out.append(right if left is None else left if right is None else left + right)
    return out


def shifted(a):
    out = [None] * (len(a) + 1)

    def put(i, value):
        out[i] = value if out[i] is None else out[i] + value

    for i, value in enumerate(a):
        if i == 0:
            put(1, value)
        else:
            put(i + 1, 0.5 * value)
            put(i - 1, 0.5 * value)
    return out


def form(a, b, gram):
    total = None
    for i, left in enumerate(a):
        inner = None
        for j, right in enumerate(b):
            if right is None:
                continue
            term = right * gram(i, j)
            inner = term if inner is None else inner + term
        inner = left * inner
        total = inner if total is None else total + inner
    return total


def recursion(moments):
    half = [0.5 * m for m in moments]

    def gram(i, j):
        return moments[i] if j == 0 else moments[j] if i == 0 else half[i + j] + half[abs(i - j)]

    one = jnp.ones_like(moments[0])
    precond, direction, head = [one], [], []
    gamma_old = alpha_old = None
    for step in range(ITERS):
        gamma = form(precond, precond, gram)
        delta = gamma - form(precond, shifted(precond), gram)
        if step == 0:
            direction = precond
            alpha = gamma / delta
        else:
            beta = gamma / gamma_old
            alpha = gamma / (delta - beta * gamma / alpha_old)
            direction = added(precond, direction, beta)
        head = added(head, direction, alpha)
        moved = added(direction, shifted(direction), -1.0)
        precond = added(precond, moved, -alpha)
        gamma_old, alpha_old = gamma, alpha
    return head, precond, added(precond, shifted(precond), -1.0)


def combine_kernel(moments, basis, inv_root, scale, strip_basis, strip_inv_root, strip_scale,
                   head_field, residual, applied, h_buf, r_buf, a_buf, sems):
    row = jnp.sum(moments[...], axis=0)
    column = lane_index(1)
    raw = []
    for n in range(2 * ITERS):
        value = jnp.sum(jnp.where(column == n, row, 0.0), axis=1, keepdims=True)
        raw.append(jnp.broadcast_to(value, (8, LANES)))
    full = raw[:2]
    for n in range(2, 2 * ITERS):
        full.append(2.0 * raw[n] - raw[n % 2])
    lane = lane_index(LAYERS)
    low, high = lane < MERGE, lane >= LANES - MERGE
    targets = (
        (h_buf, head_field, inv_root, strip_inv_root),
        (r_buf, residual, scale, strip_scale),
        (a_buf, applied, scale, strip_scale),
    )
    copies = []
    for n, (weights, (buf, out, factor, strip_factor)) in enumerate(zip(recursion(full), targets)):
        weights = [jnp.concatenate([w] * TILES, axis=0) for w in weights]

        def total(fields, factors, at):
            value = weights[0] * fields[0, at]
            for j in range(1, len(weights)):
                value = value + weights[j] * fields[j, at]
            return factors[at] * value

        strips = [total(strip_basis, strip_factor, q) for q in range(STRIPS)]
        for row in range(ROWS):
            slot, q = divmod(row + DEPTH, STRIPS)
            base = PAIR * slot
            value = total(basis, factor, row)
            value = jnp.where(low, turn(strips[q], -base - EDGE), value)
            value = jnp.where(high, turn(strips[q], LANES - (base + PAIR - EDGE)), value)
            for k in range(TILES):
                buf[pl.ds(k * ROWS + row, 8, stride=TILES * ROWS)] = value[8 * k:8 * k + 8]
        copies.append(pltpu.make_async_copy(buf, out, sems.at[n]))
        copies[-1].start()
    for copy in copies:
        copy.wait()


def f32(*shape):
    return jax.ShapeDtypeStruct(shape, jnp.float32)


def scratch(*shape):
    return pltpu.VMEM(shape, jnp.float32)


VMEM = pl.BlockSpec(memory_space=pltpu.VMEM)
HBM = pl.BlockSpec(memory_space=pltpu.HBM)


def call(kernel, outs, scratches=(), ins=VMEM, out=VMEM):
    def run(*args):
        return pl.pallas_call(
            kernel,
            out_shape=outs,
            in_specs=[ins] * len(args),
            out_specs=[out] * len(outs),
            scratch_shapes=list(scratches),
            compiler_params=pltpu.CompilerParams(vmem_limit_bytes=32 * 1024 * 1024),
        )(*args)

    return run


def prepare(recharge, conduct, top_layer, fixed_head):
    flat = (LAYERS * ROWS, LANES)
    plane = pltpu.VMEM((ROWS, LANES), jnp.int32)
    args = (recharge.reshape(flat), conduct.reshape(flat), top_layer, fixed_head)
    return call(
        prepare_kernel,
        (f32(ROWS, WIDTH, LANES), f32(FAR, LANES)),
        [scratch(*flat), scratch(*flat), plane, plane, pltpu.SemaphoreType.DMA((4,))],
        ins=HBM,
    )(*[pltpu.with_memory_space_constraint(a, pltpu.HBM) for a in args])


def near_rows(both):
    dense, strip = f32(DENSE, 8, LANES), f32(STRIPS, LAYERS, LANES)
    return call(near_kernel, (dense, dense, strip, strip, f32(8, LANES)))(both)


def edges(near, far):
    return call(edges_kernel, (f32(DENSE, 8, LANES),) * 2)(*near, far)


def own_columns(both, far, near):
    field, strip = f32(ROWS, LAYERS, LANES), f32(STRIPS, LAYERS, LANES)
    outs = (f32(BASIS, ROWS, LAYERS, LANES), field, field, f32(1, LANES), strip, strip, f32(8, LANES))
    scratches = [scratch(SPAN, WIDTH, LANES)] + [scratch(FIRST, LAYERS, LANES)] * 2
    scratches += [scratch(FIRST - 2 * j, LAYERS, LANES) for j in range(ITERS + 1)]
    return call(own_kernel, outs, scratches)(both, far, *near)


def strip_columns(moments, own, first_edge, second_edge):
    field = f32(STRIPS, LAYERS, LANES)
    outs = (f32(BASIS, STRIPS, LAYERS, LANES), field, field, f32(1, LANES))
    return call(strips_kernel, outs, [scratch(STRIPS, LAYERS, LANES)] * 3)(moments, *own, first_edge, second_edge)


def combine(moments, own, strips):
    flat = (LAYERS * ROWS, LANES)
    outs = call(
        combine_kernel,
        (f32(*flat),) * 3,
        [scratch(*flat)] * 3 + [pltpu.SemaphoreType.DMA((3,))],
        out=HBM,
    )(moments, *own, *strips)
    return tuple(out.reshape(LAYERS, ROWS, LANES) for out in outs)


def swap(array, axis, start):
    pairs = []
    for i in range(start, lax.axis_size(axis) - 1, 2):
        pairs += [(i, i + 1), (i + 1, i)]
    return lax.ppermute(array, axis, pairs)


def spread_sum(row, axes, leader):
    count = lax.axis_size(axes)
    group = [(leader + i) % count for i in range(count)]
    rows = jnp.broadcast_to(row[None], (count,) + row.shape)
    return lax.all_to_all(rows, axes, 0, 0, axis_index_groups=[group], tiled=True)


def local(recharge, conduct, top_layer, fixed_head):
    main, part = prepare(recharge, conduct, top_layer, fixed_head)
    far = swap(part, GX, 1)
    both = lax.all_gather(main, "c", axis=0, tiled=True)
    near = near_rows(both)
    first_edge, second_edge = edges(near[:2], far)
    first_edge = swap(first_edge, "y", 0)
    second_edge = swap(second_edge, "y", 1)
    *own, own_moments, root, source, fixed = own_columns(both, far, near[2:])
    *strips, moments = strip_columns(own_moments, (root, source, fixed), first_edge, second_edge)
    moments = jnp.sum(spread_sum(moments, ("z", "c"), 7 * 2 + 1), axis=0)
    moments = spread_sum(moments, ("x", "y"), 2 * 8 + 4)
    return combine(moments, own, strips)


def solution(mesh):
    grid = Mesh(mesh.devices.reshape(12, 4, 2, 8), ("z", "x", "c", "y"))
    field, plane = P(None, GX, "y"), P(GX, "y")
    return jax.shard_map(
        local, mesh=grid, in_specs=(field, field, plane, plane), out_specs=(field, field, field), check_vma=False
    )
```

```python
import jax
import jax.numpy as jnp
from jax import lax
from jax.experimental import pallas as pl
from jax.experimental.pallas import tpu as pltpu
from jax.sharding import Mesh, PartitionSpec as P

ITERS = 4
LAYERS = 48
ROWS = 8
LANES = 128
BASIS = ITERS + 2
DEPTH = BASIS
SPAN = ROWS + 2 * DEPTH
WIDTH = 2 * LAYERS + 8
TILES = LAYERS // 8
FIRST = SPAN - 2
LEAD = (FIRST - ROWS) // 2

EDGE = 7
SIDE = 3 * EDGE
PAIR = 2 * SIDE
FOLD = 3
STRIPS = 7
DENSE = 2 * STRIPS + 1
FAR = (2 * DEPTH - 1) * LAYERS + 8
MERGE = 8

store_term = 0.1
boundary_term = 4.0
vertical_ratio = 0.3

GX = ("z", "x", "c")


def lane_index(rows):
    return lax.broadcasted_iota(jnp.int32, (rows, LANES), 1)


def turn(tile, lanes):
    lanes %= LANES
    return pltpu.roll(tile, lanes, 1) if lanes else tile


def between(lane, low, high):
    return (lane >= low) & (lane < high)


def layer_above(row):
    sublane = lax.broadcasted_iota(jnp.int32, (8, LANES), 0)
    edge = jnp.where(sublane == 0, 0.0, pltpu.roll(row[LAYERS - 8:], 1, 0))
    return jnp.concatenate([edge, row[:LAYERS - 8]], axis=0)


def layer_below(row):
    sublane = lax.broadcasted_iota(jnp.int32, (8, LANES), 0)
    edge = jnp.where(sublane == 7, 0.0, pltpu.roll(row[:8], 7, 0))
    return jnp.concatenate([row[8:], edge], axis=0)


def neighbours(row, before, after):
    sides = turn(row, 1) + turn(row, -1) + before + after
    return sides + vertical_ratio * (layer_above(row) + layer_below(row))


def start_fields(root, source, fixed, total):
    head = jnp.where(layer_above(root) > 0.0, 0.0, boundary_term * fixed)
    diagonal = jnp.where(root > 0.0, root * total + (store_term + head), 1.0)
    inverse = 1.0 / diagonal
    return diagonal, root * root * inverse, source * inverse


def outer_factors(root, diagonal):
    inv = jnp.where(root > 0.0, 1.0 / root, 0.0)
    return inv, diagonal * inv


def products(weight, fields):
    out = []
    for j in range(ITERS):
        weighted = weight * fields[j]
        out += [weighted * fields[j], weighted * fields[j + 1]]
    return out


def as_row(totals):
    column = lane_index(1)
    row = jnp.zeros((1, LANES), jnp.float32)
    for n, total in enumerate(totals):
        row = jnp.where(column == n, jnp.sum(jnp.sum(total, axis=0, keepdims=True), axis=1, keepdims=True), row)
    return row


def rows_in_blocks(count, unroll, step):
    def block(k, _):
        stores = []
        for m in range(unroll):
            stores += step(k * unroll + m)
        for ref, where, value in stores:
            ref[where] = value
        return 0

    lax.fori_loop(0, count // unroll, block, 0)


def prepare_kernel(recharge, conduct, top_layer, fixed_head, main, part, r_buf, c_buf, t_buf, f_buf, sems):
    pairs = ((conduct, c_buf), (top_layer, t_buf), (recharge, r_buf), (fixed_head, f_buf))
    copies = [pltpu.make_async_copy(a, b, sems.at[n]) for n, (a, b) in enumerate(pairs)]
    for copy in copies:
        copy.start()
    core = lax.axis_index("c")
    level = TILES * lax.broadcasted_iota(jnp.int32, (8, LANES), 0)
    tiles = [(row, k, pl.ds(k * ROWS + row, 8, stride=TILES * ROWS)) for row in range(ROWS) for k in range(TILES)]
    copies[0].wait()
    copies[1].wait()
    for row, k, layers in tiles:
        root = jnp.where(level + k >= t_buf[row:row + 1], jnp.sqrt(c_buf[layers]), 0.0)
        main[row, 8 * k:8 * k + 8] = root
    nearest = [jnp.where(core == 0, n, ROWS - 1 - n) for n in range(DEPTH)]
    for n, row in enumerate(nearest):
        part[n * LAYERS:(n + 1) * LAYERS] = main[row, :LAYERS]
    copies[2].wait()
    copies[3].wait()
    for row, k, layers in tiles:
        main[row, LAYERS + 8 * k:LAYERS + 8 * k + 8] = main[row, 8 * k:8 * k + 8] * r_buf[layers]
    for n, row in enumerate(nearest[:-1]):
        part[(DEPTH + n) * LAYERS:(DEPTH + n + 1) * LAYERS] = main[row, LAYERS:2 * LAYERS]
    fixed = f_buf[...].astype(jnp.float32)
    part[FAR - 8:] = fixed
    for row in range(ROWS):
        main[row, 2 * LAYERS:] = jnp.broadcast_to(fixed[row:row + 1], (8, LANES))


def on_each_core(body):
    core = lax.axis_index("c")
    for which in range(2):
        @pl.when(core == which)
        def _(which=which):
            near = range(DEPTH, SPAN) if which == 0 else range(SPAN - DEPTH)
            body(which, near, [row for row in range(SPAN) if row not in near])


def add_units(low, high, row, read):
    lane = lane_index(8)
    sublane = lax.broadcasted_iota(jnp.int32, (8, LANES), 0)
    slot, strip = divmod(row, STRIPS)
    for unit in range(2 * TILES + 1):
        group, place = divmod(unit, TILES)
        dense, to = 2 * strip + group, PAIR * slot + EDGE * place
        if unit == 2 * TILES:
            dense, to = DENSE - 1, PAIR * slot
        back = (to - EDGE) % LANES
        take_low, take_high = between(lane, to, to + EDGE), between(lane, back, back + EDGE)
        if dense == DENSE - 1:
            take_low, take_high = take_low & (sublane == strip), take_high & (sublane == strip)
        turned = turn(read(8 * unit), to)
        for tiles, take in ((low, take_low), (high, take_high)):
            tiles[dense] = jnp.where(take, turned, 0.0 if tiles[dense] is None else tiles[dense])


def add_own(tiles, row, read):
    lane = lane_index(8)
    sublane = lax.broadcasted_iota(jnp.int32, (8, LANES), 0)
    slot, strip = divmod(row, STRIPS)
    base = PAIR * slot
    for unit in range(2 * TILES + 1):
        source = read(8 * unit)
        key = (strip, unit) if unit < 2 * TILES else None
        take_low = between(lane, base + EDGE, base + SIDE)
        take_high = between(lane, base + SIDE, base + PAIR - EDGE)
        if key is None:
            take_low, take_high = take_low & (sublane == strip), take_high & (sublane == strip)
        tile = jnp.where(take_low, turn(source, base + EDGE), tiles.get(key, 0.0))
        tiles[key] = jnp.where(take_high, turn(source, base + PAIR - EDGE), tile)


def strip_place(refs, key):
    root, source, fixed = refs
    if key is None:
        return fixed, ...
    strip, unit = key
    ref = root if unit < TILES else source
    return ref, (strip, pl.ds(8 * (unit % TILES), 8))


def near_kernel(both, low_edge, high_edge, *strip_refs):
    def body(which, near, _):
        shift = -DEPTH if which == 0 else ROWS - DEPTH
        low, high, strips = [None] * DENSE, [None] * DENSE, {}
        for row in near:
            def read(at, row=row):
                return both[row + shift, at:at + 8]

            add_units(low, high, row, read)
            add_own(strips, row, read)
        for n in range(DENSE):
            low_edge[n] = low[n]
            high_edge[n] = high[n]
        for key, tile in strips.items():
            ref, at = strip_place(strip_refs, key)
            ref[at] = tile

    on_each_core(body)


def far_row(far, which, row):
    n = DEPTH - 1 - row if which == 0 else row - ROWS - DEPTH
    at = FAR - 8 + (ROWS - 1 - n if which == 0 else n)
    root = far[n * LAYERS:(n + 1) * LAYERS]
    if n < DEPTH - 1:
        source = far[(DEPTH + n) * LAYERS:(DEPTH + n + 1) * LAYERS]
    else:
        source = jnp.zeros((LAYERS, LANES), jnp.float32)
    return jnp.concatenate([root, source, jnp.broadcast_to(far[at:at + 1], (8, LANES))], axis=0)


def edges_kernel(near_low, near_high, far, first_edge, second_edge):
    even = lax.rem(lax.axis_index("y"), 2) == 0

    def body(which, _, rows):
        low, high = [near_low[n] for n in range(DENSE)], [near_high[n] for n in range(DENSE)]
        for row in rows:
            values = far_row(far, which, row)
            add_units(low, high, row, lambda at, values=values: values[at:at + 8])
        for n in range(DENSE):
            first_edge[n] = jnp.where(even, high[n], low[n])
            second_edge[n] = jnp.where(even, low[n], high[n])

    on_each_core(body)


def own_kernel(both, far, near_root, near_source, near_fixed, basis, inv_root, scale, moments,
               strip_root, strip_source, strip_fixed, span, g, diag, *t):
    def fill(which, near, rows):
        for row in near:
            span[row] = both[row - DEPTH if which == 0 else row + ROWS - DEPTH]
        for row in rows:
            span[row] = far_row(far, which, row)

    on_each_core(fill)

    def start(i):
        row = i + 1
        root = span[row, :LAYERS]
        total = neighbours(root, span[row - 1, :LAYERS], span[row + 1, :LAYERS])
        fixed = span[row, 2 * LAYERS:2 * LAYERS + 1]
        d, g_row, t_row = start_fields(root, span[row, LAYERS:2 * LAYERS], fixed, total)
        return [(diag, i, d), (g, i, g_row), (t[0], i, t_row)]

    rows_in_blocks(FIRST, 3, start)

    for j, unroll in zip(range(1, ITERS + 1), (4, 7, 6, 5)):
        def step(i, j=j):
            new = g[i + j] * neighbours(t[j - 1][i + 1], t[j - 1][i], t[j - 1][i + 2])
            return [(t[j], i, new if j == 1 else 2.0 * new - t[j - 2][i + 2])]

        rows_in_blocks(FIRST - 2 * j, unroll, step)

    wide = lane_index(LAYERS)
    inner = between(wide, MERGE, LANES - MERGE)
    unroll = 2

    def finish(k, totals):
        stores = []
        for m in range(unroll):
            i = k * unroll + m
            fields = [t[j][i + LEAD - j] for j in range(ITERS + 1)]
            sums = neighbours(t[ITERS][i + 1], t[ITERS][i], t[ITERS][i + 2])
            fields.append(2.0 * g[i + LEAD] * sums - fields[ITERS - 1])
            inv, ratio = outer_factors(span[i + DEPTH, :LAYERS], diag[i + LEAD])
            stores += [(basis, (j, i), fields[j]) for j in range(BASIS)]
            stores += [(inv_root, i, inv), (scale, i, ratio)]
            new = products(jnp.where(inner, ratio * inv, 0.0), fields)
            totals = tuple(a + b for a, b in zip(totals, new))
        for ref, where, value in stores:
            ref[where] = value
        return totals

    zero = jnp.zeros((LAYERS, LANES), jnp.float32)
    moments[...] = as_row(lax.fori_loop(0, ROWS // unroll, finish, (zero,) * (2 * ITERS)))

    strip_root[...] = near_root[...]
    strip_source[...] = near_source[...]
    strip_fixed[...] = near_fixed[...]
    refs = (strip_root, strip_source, strip_fixed)

    def body(which, _, rows):
        keys = [(row % STRIPS, unit) for row in rows for unit in range(2 * TILES)] + [None]
        tiles = {}
        for key in keys:
            ref, at = strip_place(refs, key)
            tiles[key] = ref[at]
        for row in rows:
            add_own(tiles, row, lambda at, row=row: span[row, at:at + 8])
        for key, tile in tiles.items():
            ref, at = strip_place(refs, key)
            ref[at] = tile

    on_each_core(body)


def strips_kernel(own_moments, own_root, own_source, own_fixed, first_edge, second_edge,
                  basis, inv_root, scale, moments, root, source, g):
    lane = lane_index(8)
    low_lanes = high_lanes = lane < 0
    for slot in range(FOLD):
        base = PAIR * slot
        low_lanes = low_lanes | between(lane, base, base + EDGE)
        high_lanes = high_lanes | between(lane, base + PAIR - EDGE, base + PAIR)

    even = lax.rem(lax.axis_index("y"), 2) == 0

    def from_sides(dense):
        first, second = first_edge[dense], second_edge[dense]
        return jnp.where(even, second, first), jnp.where(even, first, second)

    def with_halo(own, sides, place=0):
        low = turn(sides[0], EDGE - EDGE * place)
        high = turn(sides[1], PAIR - EDGE - EDGE * place)
        return jnp.where(low_lanes, low, jnp.where(high_lanes, high, own))

    fixed = with_halo(own_fixed[...], from_sides(DENSE - 1))
    for q in range(STRIPS):
        root_sides, source_sides = from_sides(2 * q), from_sides(2 * q + 1)
        for k in range(TILES):
            tile = pl.ds(8 * k, 8)
            root[q, tile] = with_halo(own_root[q, tile], root_sides, k)
            source[q, tile] = with_halo(own_source[q, tile], source_sides, k)

    def sums(ref, at):
        rows = [ref[(*at, q)] for q in range(STRIPS)]
        before = [turn(rows[-1], PAIR)] + rows[:-1]
        after = rows[1:] + [turn(rows[0], -PAIR)]
        return [neighbours(*three) for three in zip(rows, before, after)]

    wide = lane_index(LAYERS)
    own_lanes = []
    for slot in range(2):
        base = PAIR * slot
        low = between(wide, base + EDGE, base + EDGE + MERGE)
        own_lanes.append(low | between(wide, base + PAIR - EDGE - MERGE, base + PAIR - EDGE))

    weights = []
    for q, total in enumerate(sums(root, ())):
        d, g[q], basis[0, q] = start_fields(root[q], source[q], fixed[q:q + 1], total)
        inv, ratio = outer_factors(root[q], d)
        inv_root[q] = inv
        scale[q] = ratio
    for j in range(1, BASIS):
        for q, total in enumerate(sums(basis, (j - 1,))):
            new = g[q] * total
            basis[j, q] = new if j == 1 else 2.0 * new - basis[j - 2, q]

    totals = None
    for q in range(STRIPS):
        mine = own_lanes[1] | own_lanes[0] if q == DEPTH else own_lanes[1]
        new = products(jnp.where(mine, scale[q] * inv_root[q], 0.0), [basis[j, q] for j in range(ITERS + 1)])
        totals = new if totals is None else [a + b for a, b in zip(totals, new)]
    moments[...] = own_moments[...] + as_row(totals)


def added(a, b, factor):
    out = []
    for i in range(max(len(a), len(b))):
        left = a[i] if i < len(a) else None
        right = b[i] if i < len(b) else None
        if right is not None:
            right = factor * right
        out.append(right if left is None else left if right is None else left + right)
    return out


def shifted(a):
    out = [None] * (len(a) + 1)

    def put(i, value):
        out[i] = value if out[i] is None else out[i] + value

    for i, value in enumerate(a):
        if i == 0:
            put(1, value)
        else:
            put(i + 1, 0.5 * value)
            put(i - 1, 0.5 * value)
    return out


def form(a, b, gram):
    total = None
    for i, left in enumerate(a):
        inner = None
        for j, right in enumerate(b):
            if right is None:
                continue
            term = right * gram(i, j)
            inner = term if inner is None else inner + term
        inner = left * inner
        total = inner if total is None else total + inner
    return total


def recursion(moments):
    half = [0.5 * m for m in moments]

    def gram(i, j):
        return moments[i] if j == 0 else moments[j] if i == 0 else half[i + j] + half[abs(i - j)]

    one = jnp.ones_like(moments[0])
    precond, direction, head = [one], [], []
    gamma_old = alpha_old = None
    for step in range(ITERS):
        gamma = form(precond, precond, gram)
        delta = gamma - form(precond, shifted(precond), gram)
        if step == 0:
            direction = precond
            alpha = gamma / delta
        else:
            beta = gamma / gamma_old
            alpha = gamma / (delta - beta * gamma / alpha_old)
            direction = added(precond, direction, beta)
        head = added(head, direction, alpha)
        moved = added(direction, shifted(direction), -1.0)
        precond = added(precond, moved, -alpha)
        gamma_old, alpha_old = gamma, alpha
    return head, precond, added(precond, shifted(precond), -1.0)


def combine_kernel(moments, basis, inv_root, scale, strip_basis, strip_inv_root, strip_scale,
                   head_field, residual, applied, h_buf, r_buf, a_buf, sems):
    row = jnp.sum(moments[...], axis=0)
    column = lane_index(1)
    raw = []
    for n in range(2 * ITERS):
        value = jnp.sum(jnp.where(column == n, row, 0.0), axis=1, keepdims=True)
        raw.append(jnp.broadcast_to(value, (8, LANES)))
    full = raw[:2]
    for n in range(2, 2 * ITERS):
        full.append(2.0 * raw[n] - raw[n % 2])
    lane = lane_index(LAYERS)
    low, high = lane < MERGE, lane >= LANES - MERGE
    targets = (
        (h_buf, head_field, inv_root, strip_inv_root),
        (r_buf, residual, scale, strip_scale),
        (a_buf, applied, scale, strip_scale),
    )
    copies = []
    for n, (weights, (buf, out, factor, strip_factor)) in enumerate(zip(recursion(full), targets)):
        weights = [jnp.concatenate([w] * TILES, axis=0) for w in weights]

        def total(fields, factors, at):
            value = weights[0] * fields[0, at]
            for j in range(1, len(weights)):
                value = value + weights[j] * fields[j, at]
            return factors[at] * value

        strips = [total(strip_basis, strip_factor, q) for q in range(STRIPS)]
        for row in range(ROWS):
            slot, q = divmod(row + DEPTH, STRIPS)
            base = PAIR * slot
            value = total(basis, factor, row)
            value = jnp.where(low, turn(strips[q], -base - EDGE), value)
            value = jnp.where(high, turn(strips[q], LANES - (base + PAIR - EDGE)), value)
            for k in range(TILES):
                buf[pl.ds(k * ROWS + row, 8, stride=TILES * ROWS)] = value[8 * k:8 * k + 8]
        copies.append(pltpu.make_async_copy(buf, out, sems.at[n]))
        copies[-1].start()
    for copy in copies:
        copy.wait()


def f32(*shape):
    return jax.ShapeDtypeStruct(shape, jnp.float32)


def scratch(*shape):
    return pltpu.VMEM(shape, jnp.float32)


VMEM = pl.BlockSpec(memory_space=pltpu.VMEM)
HBM = pl.BlockSpec(memory_space=pltpu.HBM)


def call(kernel, outs, scratches=(), ins=VMEM, out=VMEM):
    def run(*args):
        return pl.pallas_call(
            kernel,
            out_shape=outs,
            in_specs=[ins] * len(args),
            out_specs=[out] * len(outs),
            scratch_shapes=list(scratches),
            compiler_params=pltpu.CompilerParams(vmem_limit_bytes=32 * 1024 * 1024),
        )(*args)

    return run


def prepare(recharge, conduct, top_layer, fixed_head):
    flat = (LAYERS * ROWS, LANES)
    plane = pltpu.VMEM((ROWS, LANES), jnp.int32)
    args = (recharge.reshape(flat), conduct.reshape(flat), top_layer, fixed_head)
    return call(
        prepare_kernel,
        (f32(ROWS, WIDTH, LANES), f32(FAR, LANES)),
        [scratch(*flat), scratch(*flat), plane, plane, pltpu.SemaphoreType.DMA((4,))],
        ins=HBM,
    )(*[pltpu.with_memory_space_constraint(a, pltpu.HBM) for a in args])


def near_rows(both):
    dense, strip = f32(DENSE, 8, LANES), f32(STRIPS, LAYERS, LANES)
    return call(near_kernel, (dense, dense, strip, strip, f32(8, LANES)))(both)


def edges(near, far):
    return call(edges_kernel, (f32(DENSE, 8, LANES),) * 2)(*near, far)


def own_columns(both, far, near):
    field, strip = f32(ROWS, LAYERS, LANES), f32(STRIPS, LAYERS, LANES)
    outs = (f32(BASIS, ROWS, LAYERS, LANES), field, field, f32(1, LANES), strip, strip, f32(8, LANES))
    scratches = [scratch(SPAN, WIDTH, LANES)] + [scratch(FIRST, LAYERS, LANES)] * 2
    scratches += [scratch(FIRST - 2 * j, LAYERS, LANES) for j in range(ITERS + 1)]
    return call(own_kernel, outs, scratches)(both, far, *near)


def strip_columns(moments, own, first_edge, second_edge):
    field = f32(STRIPS, LAYERS, LANES)
    outs = (f32(BASIS, STRIPS, LAYERS, LANES), field, field, f32(1, LANES))
    return call(strips_kernel, outs, [scratch(STRIPS, LAYERS, LANES)] * 3)(moments, *own, first_edge, second_edge)


def combine(moments, own, strips):
    flat = (LAYERS * ROWS, LANES)
    outs = call(
        combine_kernel,
        (f32(*flat),) * 3,
        [scratch(*flat)] * 3 + [pltpu.SemaphoreType.DMA((3,))],
        out=HBM,
    )(moments, *own, *strips)
    return tuple(out.reshape(LAYERS, ROWS, LANES) for out in outs)


def swap(array, axis, start):
    pairs = []
    for i in range(start, lax.axis_size(axis) - 1, 2):
        pairs += [(i, i + 1), (i + 1, i)]
    return lax.ppermute(array, axis, pairs)


def spread_sum(row, axes, leader):
    count = lax.axis_size(axes)
    group = [(leader + i) % count for i in range(count)]
    rows = jnp.broadcast_to(row[None], (count,) + row.shape)
    return lax.all_to_all(rows, axes, 0, 0, axis_index_groups=[group], tiled=True)


def local(recharge, conduct, top_layer, fixed_head):
    main, part = prepare(recharge, conduct, top_layer, fixed_head)
    far = swap(part, GX, 1)
    both = lax.all_gather(main, "c", axis=0, tiled=True)
    near = near_rows(both)
    first_edge, second_edge = edges(near[:2], far)
    first_edge = swap(first_edge, "y", 0)
    second_edge = swap(second_edge, "y", 1)
    *own, own_moments, root, source, fixed = own_columns(both, far, near[2:])
    *strips, moments = strip_columns(own_moments, (root, source, fixed), first_edge, second_edge)
    moments = jnp.sum(spread_sum(moments, ("z", "c"), 8 * 2), axis=0)
    moments = spread_sum(moments, ("x", "y"), 2 * 8 + 4)
    return combine(moments, own, strips)


def solution(mesh):
    grid = Mesh(mesh.devices.reshape(12, 4, 2, 8), ("z", "x", "c", "y"))
    field, plane = P(None, GX, "y"), P(GX, "y")
    return jax.shard_map(
        local, mesh=grid, in_specs=(field, field, plane, plane), out_specs=(field, field, field), check_vma=False
    )
```
